512 devices in a mesh: batch: 4 (over z_lo), rows: 16 (over y, core), cols: 8 (over z_hi, x).
Axes of the slice: x: 4, y: 8, z: 8 (z_hi: 2, z_lo: 4; z = z_hi * 4 + z_lo), core: 2. Of those that a mesh axis runs over, the one named last changes fastest.
Arguments:
- features: bfloat16 [1024, 512, 1024], P(('batch', 'rows'), 'cols'), parts along dimension 0, may hold values from -6 to 6
- qkv_weight: bfloat16 [1024, 1536], replicated, may hold values from -10 to 10
- orders: int32 [64, 32, 256], P(('batch', 'rows'), 'cols'), parts along dimension 0, may hold values from 0 to 255, each once within a row
Outputs:
- attended: bfloat16 [1024, 512, 512], P(('batch', 'rows'), 'cols'), parts along dimension 0
The draws below stay inside these ranges and needn't reach their ends.
There are 4 independent parts, one for each index of `batch`. The reference program is written for one: setup_inputs(seed, part) draws one part's arguments, and reference() takes and returns one part's arrays. A program takes and returns all parts, laid end to end along the dimension named above; an argument that names none is the same for every part. Nothing has to cross between parts.
All inputs are finite; a program needn't handle non-finite values.
Results may differ from the reference program's by a relative error of at most 0.0078.
Values may be sent and summed in bfloat16 or wider, within the bound.
No kernel may reach another device: no remote copies, remote signals or barrier semaphores. Data moves between devices by JAX's collectives and lax.ppermute only.
A program may use at most 128 MiB of HBM per device.

```python
import jax
import jax.numpy as jnp
from jax import lax

D = 1024
HEADS = 8
HEAD_DIM = 64
WINDOW = 16
HALF_WINDOW = 8
GRID_ROWS = 256
GRID_COLS = 512
ALL_WIN_ROWS = 16
ALL_WIN_COLS = 32
TOKEN_WIN = 256
INNER_DIM = 512


def draw_qkv_weight(key, part):
    key = jax.random.fold_in(key, 7)
    base = jax.random.truncated_normal(key, -4.0, 4.0, (D, 3 * INNER_DIM), jnp.float32) * D ** (-0.5)
    return base.astype(jnp.bfloat16)


def shard_levels(key, extent, shards, least, top_value):
    def one(dim, parts):
        heights = jax.random.uniform(jax.random.fold_in(jax.random.fold_in(key, 6), dim), (parts,), jnp.float32, least / len(shards), top_value / len(shards))
        return jnp.repeat(jnp.exp(heights), extent[dim] // parts).reshape((-1,) + (1,) * (len(extent) - dim - 1))

    level = one(*shards[0])
    for cut in shards[1:]:
        level = level * one(*cut)
    return level


def centred(rng, extent, width, most, cuts=(), held_as=jnp.bfloat16):
    factor_of = shard_levels(rng, extent, cuts, -0.22, 0.18) if cuts else 1.0
    drawn = jax.random.normal(rng, extent, jnp.float32) * width * factor_of
    return jnp.minimum(jnp.maximum(drawn, -most), most).astype(held_as)


def setup_inputs(seed: int = 0, part: int = 0) -> dict:
    arg_keys = jax.random.split(jax.random.key(seed), 4)
    part_splits = jax.random.split(jax.random.fold_in(arg_keys[3], part), 4)
    return {
        "features": centred(part_splits[0], (GRID_ROWS, GRID_COLS, D), 1.0, 6.0, ((0, 16), (1, 8))),
        "qkv_weight": draw_qkv_weight(jax.random.fold_in(arg_keys[3], 71), part),
        "orders": jax.vmap(lambda own: jax.random.permutation(own, TOKEN_WIN))(jax.random.split(part_splits[2], ALL_WIN_ROWS * ALL_WIN_COLS)).reshape((ALL_WIN_ROWS, ALL_WIN_COLS, TOKEN_WIN)).astype(jnp.int32),
    }


EPSILON = 1e-06

def normalize(values):
    widened = values.astype(jnp.float32)
    center = lax.optimization_barrier(jnp.mean(widened, axis=-1, keepdims=True))
    spread = lax.optimization_barrier(jnp.mean(jnp.square(widened - center), axis=-1, keepdims=True))
    return ((widened - center) * lax.rsqrt(spread + EPSILON)).astype(jnp.bfloat16)

def window_labels(first_row, first_col, win_down, win_across, total_rows, total_cols):
    row_index = (first_row + jnp.arange(win_down, dtype=jnp.int32)) % total_rows
    col_index = (first_col + jnp.arange(win_across, dtype=jnp.int32)) % total_cols
    row_last = row_index == total_rows - 1
    col_last = col_index == total_cols - 1
    position = jnp.arange(TOKEN_WIN, dtype=jnp.int32)
    lower_half = position // WINDOW >= HALF_WINDOW
    right_half = position % WINDOW >= HALF_WINDOW
    row_label = (row_last[:, None, None] & lower_half[None, None, :]).astype(jnp.int32)
    col_label = (col_last[None, :, None] & right_half[None, None, :]).astype(jnp.int32)
    return (2 * row_label + col_label).reshape(win_down * win_across, TOKEN_WIN)

def attend_windows(blocks, qkv_weight, orders, labels):
    count = blocks.shape[0]
    packed = jnp.dot(blocks.reshape(-1, D), qkv_weight, preferred_element_type=jnp.float32).astype(jnp.bfloat16)
    packed = packed.reshape(count, TOKEN_WIN, 3, HEADS, HEAD_DIM).astype(jnp.float32)
    query_heads = packed[:, :, 0]
    key_heads = packed[:, :, 1]
    value_heads = packed[:, :, 2]
    scores = jnp.einsum('wqhd,wkhd->whqk', query_heads, key_heads) * HEAD_DIM ** (-0.5)
    allowed = (orders[:, None, :] <= orders[:, :, None]) & (labels[:, None, :] == labels[:, :, None])
    masked = jnp.where(allowed[:, None], scores, -jnp.inf)
    row_max = lax.optimization_barrier(jnp.max(masked, axis=-1, keepdims=True))
    lifted = jnp.exp(masked - row_max)
    weights = (lifted / lax.optimization_barrier(jnp.sum(lifted, axis=-1, keepdims=True))).astype(jnp.bfloat16)
    mixed = jnp.einsum('whqk,wkhd->wqhd', weights.astype(jnp.float32), value_heads)
    return mixed.astype(jnp.bfloat16).reshape(count, TOKEN_WIN, INNER_DIM)

def reference(features, qkv_weight, orders):
    rolled = jnp.roll(features, (-HALF_WINDOW, -HALF_WINDOW), axis=(0, 1))
    normed = normalize(rolled)
    blocks = normed.reshape(ALL_WIN_ROWS, WINDOW, ALL_WIN_COLS, WINDOW, D)
    blocks = blocks.transpose(0, 2, 1, 3, 4).reshape(ALL_WIN_ROWS, ALL_WIN_COLS, TOKEN_WIN, D)

    def one_row(packed_row):
        row_number, row_blocks, row_orders = packed_row
        labels = window_labels(row_number, 0, 1, ALL_WIN_COLS, ALL_WIN_ROWS, ALL_WIN_COLS)
        return attend_windows(row_blocks, qkv_weight, row_orders, labels)
    result = lax.map(one_row, (jnp.arange(ALL_WIN_ROWS, dtype=jnp.int32), blocks, orders))
    result = result.reshape(ALL_WIN_ROWS, ALL_WIN_COLS, WINDOW, WINDOW, INNER_DIM)
    result = result.transpose(0, 2, 1, 3, 4).reshape(GRID_ROWS, GRID_COLS, INNER_DIM)
    return jnp.roll(result, (HALF_WINDOW, HALF_WINDOW), axis=(0, 1))
```

```python
import jax
import jax.numpy as jnp
from jax import lax
from jax.experimental import pallas as pl
from jax.experimental.pallas import tpu as pltpu
from jax.sharding import PartitionSpec as P

D = 1024
HEADS = 8
HEAD_DIM = 64
INNER = 512
HALF = 8
EPSILON = 1e-06
LOG2E = 1.4426950408889634
FAR = 4096.0
BF = jnp.bfloat16
F32 = jnp.float32
MIB = 1 << 20


def normalize(values):
    center = jnp.mean(values, axis=-1, keepdims=True)
    off = values - center
    spread = jnp.mean(off * off, axis=-1, keepdims=True)
    return off * lax.rsqrt(spread + EPSILON)


def pack_kernel(x_ref, ord_ref, up_a, up_b, dn_a, dn_b, e1, e2):
    odd = lax.rem(lax.axis_index("cols"), 2) == 1
    for h, (a_ref, b_ref) in enumerate(((up_a, up_b), (dn_a, dn_b))):

        def two_rows(t, _, h=h, a_ref=a_ref, b_ref=b_ref):
            rows = [x_ref[h * HALF + 2 * t + u].astype(F32) for u in range(2)]
            for j in range(3):
                for u in range(2):
                    part = normalize(rows[u][8 + 16 * j : 24 + 16 * j]).astype(BF)
                    ref, base = (a_ref, 128 * j) if j < 2 else (b_ref, 0)
                    ref[pl.ds(pl.multiple_of(base + (2 * t + u) * 16, 16), 16), :] = part
            left = normalize(jnp.concatenate([rows[0][:8], rows[1][:8]], axis=0)).astype(BF)
            right = normalize(jnp.concatenate([rows[0][56:], rows[1][56:]], axis=0)).astype(BF)
            b_ref[pl.ds(pl.multiple_of(128 + t * 16, 16), 16), :] = left
            b_ref[pl.ds(pl.multiple_of(192 + t * 16, 16), 16), :] = right
            at = pl.ds(pl.multiple_of(64 * h + t * 16, 16), 16)
            e1[at, :] = jnp.where(odd, right, left)
            e2[at, :] = jnp.where(odd, left, right)
            return 0

        lax.fori_loop(0, 4, two_rows, 0)
    ranks = ord_ref[0].astype(F32).astype(BF)
    natural = lax.broadcasted_iota(jnp.int32, (256, 256), 0)
    m = lax.broadcasted_iota(jnp.int32, (256, 256), 1)
    source = ((m >> 7) * 8 + ((m >> 3) & 7)) * 16 + ((m >> 6) & 1) * 8 + (m & 7)
    quads = jnp.dot(ranks, (natural == source).astype(F32).astype(BF), preferred_element_type=F32)
    rank_row = jnp.concatenate(
        [ranks[0:1].astype(F32), ranks[1:2].astype(F32), ranks[2:3].astype(F32), quads[3:4]], axis=1
    )
    block = jnp.broadcast_to(rank_row, (16, D)).astype(BF)
    dn_a[256:272, :] = block
    e1[128:144, :] = block
    e2[128:144, :] = block


def project_kernel(ua, ub, da, db, w_ref, pa, pb):
    for h, (a_ref, b_ref) in enumerate(((ua, ub), (da, db))):
        for src, dst in ((a_ref, pa), (b_ref, pb)):
            dst[h] = jnp.dot(src[0:256, :], w_ref[...], preferred_element_type=F32).astype(BF)


def column_of(row, count):
    q = lax.broadcasted_iota(jnp.int32, (count, 128), 0)
    lane = lax.broadcasted_iota(jnp.int32, (count, 128), 1)
    return jnp.sum(jnp.where(q == lane, jnp.broadcast_to(row, (count, 128)), 0.0), axis=1, keepdims=True)


def attend(query, keys, values, allowed):
    count = query.shape[0]
    both = jnp.concatenate([allowed, allowed], axis=0)
    first = lax.broadcasted_iota(jnp.int32, (count, 128), 1) < HEAD_DIM
    ones = jnp.ones((256, 128), BF)
    outs = []
    for g in range(4):
        at = slice(128 * g, 128 * g + 128)
        q = query[:, at]
        zero = jnp.zeros_like(q)
        q = jnp.concatenate([jnp.where(first, q, zero), jnp.where(first, zero, q)], axis=0)
        s = lax.dot_general(q, keys[:, at], (((1,), (1,)), ((), ())), preferred_element_type=F32)
        s = jnp.where(both, s, -jnp.inf)
        top = jnp.max(s, axis=-1, keepdims=True)
        p = jnp.exp2((s - top) * (LOG2E * HEAD_DIM**-0.5)).astype(BF)
        o = jnp.dot(p, jnp.concatenate([values[:, at], ones], axis=1), preferred_element_type=F32)
        number = jnp.where(first, o[:count, :128], o[count:, :128])
        total = jnp.where(first, o[:count, 128:], o[count:, 128:])
        outs.append(number / total)
    return jnp.concatenate(outs, axis=1)


def inner_window(h, j, own, other_kv, rank_row, last, out):
    own_ranks = rank_row[:, 128:] if h == 0 else rank_row[:, :128]
    other_ranks = (rank_row[:, :128] if h == 0 else rank_row[:, 128:]) + jnp.where(last, FAR, 0.0)
    key_ranks = jnp.concatenate([own_ranks, other_ranks], axis=1)
    allowed = key_ranks <= column_of(own_ranks, 128)
    keys = jnp.concatenate([own[:, INNER : 2 * INNER], other_kv[:, :INNER]], axis=0)
    values = jnp.concatenate([own[:, 2 * INNER :], other_kv[:, INNER:]], axis=0)
    out[h, j] = attend(own[:, :INNER], keys, values, allowed).astype(BF)


def last_pair(h):
    size = lax.axis_size("rows")
    return lax.axis_index("rows") == (0 if h == 0 else size - 1)


def inner_a_kernel(up_a, dn_a, pa, w_ref, ord_ref, oa):
    for h, src in enumerate((dn_a, up_a)):
        kv = jnp.dot(src[0:256, :], w_ref[:, INNER:], preferred_element_type=F32).astype(BF)
        for j in range(2):
            if h == 0:
                ranks = dn_a[256:272, 256 * j : 256 * j + 256].astype(F32)[0:1]
            else:
                ranks = ord_ref[0, j : j + 1, :].astype(F32)
            at = slice(128 * j, 128 * j + 128)
            inner_window(h, j, pa[h, at, :], kv[at], ranks, last_pair(h), oa)


def inner_b_kernel(up_b, dn_b, dn_a, pb, w_ref, ord_ref, ob, kve):
    for h, src in enumerate((dn_b, up_b)):
        kv = jnp.dot(src[0:256, :], w_ref[:, INNER:], preferred_element_type=F32).astype(BF)
        if h == 0:
            ranks = dn_a[256:272, 512:768].astype(F32)[0:1]
        else:
            ranks = ord_ref[0, 2:3, :].astype(F32)
        inner_window(h, 0, pb[h, 0:128, :], kv[0:128], ranks, last_pair(h), ob)
        kve[h, 0] = kv[128:192]
        kve[h, 1] = kv[192:256]


def strips_kernel(e1, e2, w_ref, kvf):
    for e, src in enumerate((e1, e2)):
        kv = jnp.dot(src[0:128, :], w_ref[:, INNER:], preferred_element_type=F32).astype(BF)
        kvf[e, 0] = kv[0:64]
        kvf[e, 1] = kv[64:128]


def edge_kernel(hop_u, hop_d, e1, e2, dn_a, pb, kve, kvf, oa, ob, w_ref, ord_ref, out, edge):
    col = lax.axis_index("cols")
    odd = lax.rem(col, 2)
    natural = lax.broadcasted_iota(jnp.int32, (256, 256), 0)
    m = lax.broadcasted_iota(jnp.int32, (256, 256), 1)
    source = ((m >> 7) * 8 + ((m >> 3) & 7)) * 16 + ((m >> 6) & 1) * 8 + (m & 7)
    own_ranks = ord_ref[0].astype(F32).astype(BF)
    mine = jnp.dot(own_ranks, (natural == source).astype(F32).astype(BF), preferred_element_type=F32)[3:4]
    above = dn_a[256:272, 768:1024].astype(F32)[0:1]
    diag = jnp.concatenate([hop_d[0:64, :], hop_d[80:144, :], hop_u[0:128, :]], axis=0)
    kvd = jnp.dot(diag, w_ref[:, INNER:], preferred_element_type=F32).astype(BF)
    for e, strip in enumerate((e1, e2)):
        side = odd if e == 0 else 1 - odd
        is_left = side == 0
        beside = strip[128:144, 768:1024].astype(F32)[0:1]
        corner = hop_d[80 * e + 64 : 80 * e + 80, 768:1024].astype(F32)[0:1]
        last_col = jnp.where(is_left, col == 0, col == lax.axis_size("cols") - 1)
        for h in range(2):
            ranks = jnp.where(is_left, corner, above) if h == 0 else jnp.where(is_left, beside, mine)
            half_own = ranks[:, 128:] if h == 0 else ranks[:, :128]
            half_other = ranks[:, :128] if h == 0 else ranks[:, 128:]
            half_own = jnp.where(is_left, jnp.concatenate([half_own[:, 64:], half_own[:, :64]], axis=1), half_own)
            half_other = jnp.where(is_left, jnp.concatenate([half_other[:, 64:], half_other[:, :64]], axis=1), half_other)
            lane = lax.broadcasted_iota(jnp.int32, (1, 128), 1)
            far_col = jnp.where((lane >= 64) & last_col, FAR, 0.0)
            key_ranks = jnp.concatenate(
                [half_own + far_col, half_other + far_col + jnp.where(last_pair(h), FAR, 0.0)], axis=1
            )
            allowed = key_ranks <= column_of(half_own, 64)
            own = pb[h, pl.ds(pl.multiple_of(128 + 64 * side, 64), 64), :]
            near = kve[h, side]
            far = kvf[e, h]
            cross = kvd[128 * h + 64 * e : 128 * h + 64 * e + 64]
            keys = jnp.concatenate([own[:, INNER : 2 * INNER], far[:, :INNER], near[:, :INNER], cross[:, :INNER]], axis=0)
            values = jnp.concatenate([own[:, 2 * INNER :], far[:, INNER:], near[:, INNER:], cross[:, INNER:]], axis=0)
            edge[h, side] = attend(own[:, :INNER], keys, values, allowed)
    for h in range(2):
        for i in range(HALF):
            row = jnp.concatenate(
                [
                    edge[h, 0, 8 * i : 8 * i + 8],
                    oa[h, 0, 16 * i : 16 * i + 16].astype(F32),
                    oa[h, 1, 16 * i : 16 * i + 16].astype(F32),
                    ob[h, 0, 16 * i : 16 * i + 16].astype(F32),
                    edge[h, 1, 8 * i : 8 * i + 8],
                ],
                axis=0,
            )
            out[h * HALF + i] = row.astype(BF)


def call(kernel, outs, args, flops, scratch=(), limit=40):
    sizes = sum(a.size * a.dtype.itemsize for a in args) + sum(o.size * o.dtype.itemsize for o in outs)
    single = len(outs) == 1
    vmem = pl.BlockSpec(memory_space=pltpu.VMEM)
    return pl.pallas_call(
        kernel,
        out_shape=outs[0] if single else tuple(outs),
        in_specs=[vmem] * len(args),
        out_specs=vmem if single else tuple([vmem] * len(outs)),
        scratch_shapes=list(scratch),
        compiler_params=pltpu.CompilerParams(vmem_limit_bytes=limit * MIB),
        cost_estimate=pl.CostEstimate(flops=flops, bytes_accessed=sizes, transcendentals=0),
    )(*args)


def arr(*shape):
    return jax.ShapeDtypeStruct(shape, BF)


def along_rows(value, by):
    size = lax.axis_size("rows")
    return lax.ppermute(value, "rows", [(i, (i + by) % size) for i in range(size)])


def per_device(features, qkv_weight, orders):
    cols = lax.axis_size("cols")
    up_a, up_b, dn_a, dn_b, e1, e2 = call(
        pack_kernel,
        [arr(256, D), arr(256, D), arr(272, D), arr(256, D), arr(144, D), arr(144, D)],
        [features, orders],
        20_000_000,
    )
    first = [(c, (c + 1) % cols if c % 2 else (c - 1) % cols) for c in range(cols)]
    second = [(c, (c - 1) % cols if c % 2 else (c + 1) % cols) for c in range(cols)]
    got_e1 = lax.ppermute(e1, "cols", first)
    got_up_a = along_rows(up_a, -1)
    got_dn_a = along_rows(dn_a, 1)
    got_up_b = along_rows(up_b, -1)
    got_dn_b = along_rows(dn_b, 1)
    got_e2 = lax.ppermute(e2, "cols", second)
    pa, pb = call(
        project_kernel, [arr(2, 256, 3 * INNER)] * 2, [up_a, up_b, dn_a, dn_b, qkv_weight], 3_200_000_000
    )
    oa = call(
        inner_a_kernel, [arr(2, 2, 128, INNER)], [got_up_a, got_dn_a, pa, qkv_weight, orders], 4_000_000_000
    )
    ob, kve = call(
        inner_b_kernel,
        [arr(2, 1, 128, INNER), arr(2, 2, 64, 2 * INNER)],
        [got_up_b, got_dn_b, got_dn_a, pb, qkv_weight, orders],
        3_000_000_000,
    )
    hop_u = along_rows(jnp.concatenate([got_e1[0:64], got_e2[0:64]], axis=0), -1)
    hop_d = along_rows(jnp.concatenate([got_e1[64:144], got_e2[64:144]], axis=0), 1)
    kvf = call(strips_kernel, [arr(2, 2, 64, 2 * INNER)], [got_e1, got_e2, qkv_weight], 600_000_000)
    return call(
        edge_kernel,
        [arr(16, 64, INNER)],
        [hop_u, hop_d, got_e1, got_e2, got_dn_a, pb, kve, kvf, oa, ob, qkv_weight, orders],
        2_000_000_000,
        scratch=[pltpu.VMEM((2, 2, 64, INNER), F32)],
    )


def solution(mesh):
    in_specs = (P(("batch", "rows"), "cols", None), P(), P(("batch", "rows"), "cols", None))
    out_specs = P(("batch", "rows"), "cols", None)
    return jax.shard_map(
        per_device, mesh=mesh, in_specs=in_specs, out_specs=out_specs, check_vma=False
    )
```

```python
import functools

import jax
import jax.numpy as jnp
from jax import lax
from jax.experimental import pallas as pl
from jax.experimental.pallas import tpu as pltpu
from jax.sharding import PartitionSpec as P

D = 1024
HEADS = 8
HEAD_DIM = 64
INNER = 512
HALF = 8
EPSILON = 1e-06
LOG2E = 1.4426950408889634
FAR = 4096.0
BF = jnp.bfloat16
F32 = jnp.float32
MIB = 1 << 20


def normalize(values):
    center = jnp.mean(values, axis=-1, keepdims=True)
    off = values - center
    spread = jnp.mean(off * off, axis=-1, keepdims=True)
    return off * lax.rsqrt(spread + EPSILON)


def store_ranks(ord_ref, block_refs):
    ranks = ord_ref[0].astype(F32).astype(BF)
    natural = lax.broadcasted_iota(jnp.int32, (256, 256), 0)
    m = lax.broadcasted_iota(jnp.int32, (256, 256), 1)
    source = ((m >> 7) * 8 + ((m >> 3) & 7)) * 16 + ((m >> 6) & 1) * 8 + (m & 7)
    quads = jnp.dot(ranks, (natural == source).astype(F32).astype(BF), preferred_element_type=F32)
    rank_row = jnp.concatenate(
        [ranks[0:1].astype(F32), ranks[1:2].astype(F32), ranks[2:3].astype(F32), quads[3:4]], axis=1
    )
    block = jnp.broadcast_to(rank_row, (16, D)).astype(BF)
    for ref, at in block_refs:
        ref[at : at + 16, :] = block


def put_strips(odd, at, left, right, e1, e2):
    e1[at : at + 16, :] = jnp.where(odd, right, left)
    e2[at : at + 16, :] = jnp.where(odd, left, right)


def pack_rows(x_ref, ord_hbm, up, dn, held, ord_ref, sem, strips=()):
    odd = lax.rem(lax.axis_index("cols"), 2) == 1
    copies = [
        pltpu.make_async_copy(x_ref.at[pl.ds(2 * q, 2)], held.at[pl.ds(2 * q, 2)], sem.at[q]) for q in range(8)
    ]
    ranks_copy = pltpu.make_async_copy(ord_hbm, ord_ref, sem.at[8])
    ranks_copy.start()
    for copy in copies:
        copy.start()
    ranks_copy.wait()
    store_ranks(ord_ref, [(dn, 512)] + [(ref, 128) for ref in strips])
    for q, copy in enumerate(copies):
        copy.wait()
        h, t = q // 4, q % 4
        ref = dn if h else up
        rows = [held[2 * q + u].astype(F32) for u in range(2)]
        for j in range(3):
            for u in range(2):
                part = normalize(rows[u][8 + 16 * j : 24 + 16 * j]).astype(BF)
                at = 128 * j + (2 * t + u) * 16
                ref[at : at + 16, :] = part
        left = normalize(jnp.concatenate([rows[0][:8], rows[1][:8]], axis=0)).astype(BF)
        right = normalize(jnp.concatenate([rows[0][56:], rows[1][56:]], axis=0)).astype(BF)
        ref[384 + t * 16 : 400 + t * 16, :] = left
        ref[448 + t * 16 : 464 + t * 16, :] = right
        if strips:
            put_strips(odd, 64 * h + t * 16, left, right, *strips)


def pack_kernel(x_ref, ord_hbm, up, dn, e1, e2, held, ord_ref, sem):
    pack_rows(x_ref, ord_hbm, up, dn, held, ord_ref, sem, (e1, e2))


def is_early():
    return lax.axis_index("cols") < lax.axis_size("cols") // 2


def project_early_kernel(up, dn, e1, e2, w_hbm, p, again, w_ref, sem):
    @pl.when(jnp.logical_not(is_early()))
    def _():
        again[...] = e2[...]

    @pl.when(is_early())
    def _():
        again[...] = e1[...]
        copies = []
        for n in range(3):
            at = pl.ds(INNER * n, INNER)
            copies.append(pltpu.make_async_copy(w_hbm.at[:, at], w_ref.at[:, at], sem.at[n]))
        for copy in copies:
            copy.start()
        for n, copy in enumerate(copies):
            copy.wait()
            at = slice(INNER * n, INNER * n + INNER)
            for h, src in enumerate((up, dn)):
                p[h, :, at] = jnp.dot(src[0:512, :], w_ref[:, at], preferred_element_type=F32).astype(BF)


def project_late_kernel(up, dn, w_ref, p):
    @pl.when(jnp.logical_not(is_early()))
    def _():
        for h, src in enumerate((up, dn)):
            for q in range(2):
                at = slice(256 * q, 256 * q + 256)
                p[h, at, :] = jnp.dot(src[at, :], w_ref[...], preferred_element_type=F32).astype(BF)


def column_of(row, count):
    q = lax.broadcasted_iota(jnp.int32, (count, 128), 0)
    lane = lax.broadcasted_iota(jnp.int32, (count, 128), 1)
    return jnp.sum(jnp.where(q == lane, jnp.broadcast_to(row, (count, 128)), 0.0), axis=1, keepdims=True)


def attend(query, keys, values, allowed):
    count = query.shape[0]
    both = jnp.concatenate([allowed, allowed], axis=0)
    first = lax.broadcasted_iota(jnp.int32, (count, 128), 1) < HEAD_DIM
    ones = jnp.ones((256, 128), BF)
    outs = []
    for g in range(4):
        at = slice(128 * g, 128 * g + 128)
        q = query[:, at]
        zero = jnp.zeros_like(q)
        q = jnp.concatenate([jnp.where(first, q, zero), jnp.where(first, zero, q)], axis=0)
        s = lax.dot_general(q, keys[:, at], (((1,), (1,)), ((), ())), preferred_element_type=F32)
        s = jnp.where(both, s, -jnp.inf)
        top = jnp.max(s, axis=-1, keepdims=True)
        p = jnp.exp2((s - top) * (LOG2E * HEAD_DIM**-0.5)).astype(BF)
        o = jnp.dot(p, jnp.concatenate([values[:, at], ones], axis=1), preferred_element_type=F32)
        number = jnp.where(first, o[:count, :128], o[count:, :128])
        total = jnp.where(first, o[:count, 128:], o[count:, 128:])
        outs.append(number / total)
    return jnp.concatenate(outs, axis=1)


def inner_window(h, j, own, other_kv, rank_row, last, out):
    own_ranks = rank_row[:, 128:] if h == 0 else rank_row[:, :128]
    other_ranks = (rank_row[:, :128] if h == 0 else rank_row[:, 128:]) + jnp.where(last, FAR, 0.0)
    key_ranks = jnp.concatenate([own_ranks, other_ranks], axis=1)
    allowed = key_ranks <= column_of(own_ranks, 128)
    keys = jnp.concatenate([own[:, INNER : 2 * INNER], other_kv[:, :INNER]], axis=0)
    values = jnp.concatenate([own[:, 2 * INNER :], other_kv[:, INNER:]], axis=0)
    out[h, j] = attend(own[:, :INNER], keys, values, allowed).astype(BF)


def last_pair(h):
    size = lax.axis_size("rows")
    return lax.axis_index("rows") == (0 if h == 0 else size - 1)


def by_side(body, p_early, p_late):
    early = is_early()
    pl.when(early)(lambda: body(p_early))
    pl.when(jnp.logical_not(early))(lambda: body(p_late))


def inner_kernel(up, dn, p_early, p_late, w_ref, ord_ref, out, kve):
    by_side(lambda p: inner_windows(up, dn, p, w_ref, ord_ref, out, kve), p_early, p_late)


def inner_windows(up, dn, p, w_ref, ord_ref, out, kve):
    for h, src in enumerate((dn, up)):
        kv = jnp.dot(src[0:512, :], w_ref[:, INNER:], preferred_element_type=F32).astype(BF)
        for j in range(3):
            if h == 0:
                ranks = dn[512:528, 256 * j : 256 * j + 256].astype(F32)[0:1]
            else:
                ranks = ord_ref[0, j : j + 1, :].astype(F32)
            at = slice(128 * j, 128 * j + 128)
            inner_window(h, j, p[h, at, :], kv[at], ranks, last_pair(h), out)
        kve[h, 0] = kv[384:448]
        kve[h, 1] = kv[448:512]


def one_of(cols):
    col = lax.axis_index("cols")
    return functools.reduce(jnp.logical_or, [col == c for c in cols])


def merge_kernel(got_x, got_z, tie, to_up, to_dn):
    del tie
    for e, src in enumerate((got_x, got_z)):
        to_up[64 * e : 64 * e + 64, :] = src[0:64, :]
        to_dn[80 * e : 80 * e + 80, :] = src[64:144, :]


def split_kernel(got_y, tie, to_up, to_dn):
    del tie
    to_up[...] = got_y[0:64, :]
    to_dn[...] = got_y[64:144, :]


def strips_kernel(y_first, y_second, got_x, got_y, got_z, w_ref, tie, kvf):
    del tie
    for e, (src, y_cols) in enumerate(((got_x, y_first), (got_z, y_second))):
        strip = jnp.where(one_of(y_cols), got_y[0:128, :], src[0:128, :])
        kv = jnp.dot(strip, w_ref[:, INNER:], preferred_element_type=F32).astype(BF)
        kvf[e, 0] = kv[0:64]
        kvf[e, 1] = kv[64:128]


def edge_kernel(y_first, y_second, *refs):
    ux, uy, dx, dy, got_x, got_y, got_z, kvf, w_ref, ord_ref = refs[:10]
    dn, p_early, p_late, inner, kve, out, edge = refs[10:]
    ups, downs, besides, corners = [], [], [], []
    for e, (src, y_cols) in enumerate(((got_x, y_first), (got_z, y_second))):
        from_y = one_of(y_cols)
        ups.append(jnp.where(from_y, uy[...], ux[64 * e : 64 * e + 64, :]))
        downs.append(jnp.where(from_y, dy[0:64, :], dx[80 * e : 80 * e + 64, :]))
        corners.append(jnp.where(from_y, dy[64:80, 768:1024], dx[80 * e + 64 : 80 * e + 80, 768:1024]))
        besides.append(jnp.where(from_y, got_y[128:144, 768:1024], src[128:144, 768:1024]))
    col = lax.axis_index("cols")
    odd = lax.rem(col, 2)
    natural = lax.broadcasted_iota(jnp.int32, (256, 256), 0)
    m = lax.broadcasted_iota(jnp.int32, (256, 256), 1)
    source = ((m >> 7) * 8 + ((m >> 3) & 7)) * 16 + ((m >> 6) & 1) * 8 + (m & 7)
    own_ranks = ord_ref[0].astype(F32).astype(BF)
    mine = jnp.dot(own_ranks, (natural == source).astype(F32).astype(BF), preferred_element_type=F32)[3:4]
    diag = jnp.concatenate(downs + ups, axis=0)
    kvd = jnp.dot(diag, w_ref[:, INNER:], preferred_element_type=F32).astype(BF)

    def edges(p):
        above = dn[512:528, 768:1024].astype(F32)[0:1]
        for e, (beside, corner) in enumerate(zip(besides, corners)):
            side = odd if e == 0 else 1 - odd
            is_left = side == 0
            beside = beside.astype(F32)[0:1]
            corner = corner.astype(F32)[0:1]
            last_col = jnp.where(is_left, col == 0, col == lax.axis_size("cols") - 1)
            for h in range(2):
                ranks = jnp.where(is_left, corner, above) if h == 0 else jnp.where(is_left, beside, mine)
                half_own = ranks[:, 128:] if h == 0 else ranks[:, :128]
                half_other = ranks[:, :128] if h == 0 else ranks[:, 128:]
                half_own, half_other = (
                    jnp.where(is_left, jnp.concatenate([x[:, 64:], x[:, :64]], axis=1), x) for x in (half_own, half_other)
                )
                lane = lax.broadcasted_iota(jnp.int32, (1, 128), 1)
                far_col = jnp.where((lane >= 64) & last_col, FAR, 0.0)
                key_ranks = jnp.concatenate(
                    [half_own + far_col, half_other + far_col + jnp.where(last_pair(h), FAR, 0.0)], axis=1
                )
                allowed = key_ranks <= column_of(half_own, 64)
                own = p[h, pl.ds(pl.multiple_of(384 + 64 * side, 64), 64), :]
                near = kve[h, side]
                far = kvf[e, h]
                cross = kvd[128 * h + 64 * e : 128 * h + 64 * e + 64]
                keys = jnp.concatenate(
                    [own[:, INNER : 2 * INNER], far[:, :INNER], near[:, :INNER], cross[:, :INNER]], axis=0
                )
                values = jnp.concatenate([own[:, 2 * INNER :], far[:, INNER:], near[:, INNER:], cross[:, INNER:]], axis=0)
                edge[h, side] = attend(own[:, :INNER], keys, values, allowed)

        for h in range(2):
            for i in range(HALF):
                row = [edge[h, 0, 8 * i : 8 * i + 8]]
                row += [inner[h, j, 16 * i : 16 * i + 16].astype(F32) for j in range(3)]
                row += [edge[h, 1, 8 * i : 8 * i + 8]]
                out[h * HALF + i] = jnp.concatenate(row, axis=0).astype(BF)

    by_side(edges, p_early, p_late)


STRIP_FLOPS = 1000
VMEM = pl.BlockSpec(memory_space=pltpu.VMEM)
ANY = pl.BlockSpec(memory_space=pl.ANY)
HBM = pl.BlockSpec(memory_space=pltpu.HBM)


def call(kernel, outs, args, flops, anywhere=(), scratch=(), aliases=None, limit=24, held=()):
    single = len(outs) == 1
    return pl.pallas_call(
        kernel,
        out_shape=outs[0] if single else tuple(outs),
        in_specs=[HBM if i in held else ANY if i in anywhere else VMEM for i in range(len(args))],
        out_specs=VMEM if single else tuple([VMEM] * len(outs)),
        scratch_shapes=list(scratch),
        input_output_aliases=aliases or {},
        compiler_params=pltpu.CompilerParams(vmem_limit_bytes=limit * MIB),
        cost_estimate=pl.CostEstimate(flops=flops, bytes_accessed=1_000, transcendentals=0),
    )(*args)


def arr(*shape):
    return jax.ShapeDtypeStruct(shape, BF)


def along_rows(value, by):
    size = lax.axis_size("rows")
    return lax.ppermute(value, "rows", [(i, (i + by) % size) for i in range(size)])


def fixed(x):
    return pltpu.with_memory_space_constraint(x, pltpu.HBM)


def per_device(features, qkv_weight, orders):
    cols = lax.axis_size("cols")
    half = cols // 2
    up, dn, e1, e2 = call(
        pack_kernel,
        [arr(512, D), arr(528, D), arr(144, D), arr(144, D)],
        [fixed(features), fixed(orders)],
        1_000,
        held=(0, 1),
        scratch=[pltpu.VMEM((16, 64, D), BF), pltpu.VMEM((1, 4, 256), jnp.int32), pltpu.SemaphoreType.DMA((9,))],
        limit=16,
    )
    first = [(c, (c + 1) % cols if c % 2 else (c - 1) % cols) for c in range(cols)]
    second = [(c, (c - 1) % cols if c % 2 else (c + 1) % cols) for c in range(cols)]
    to_late = [(a, b) for a, b in first if a < half <= b]
    far = [b for _, b in to_late]
    from_far = [(a, b) for a, b in second if a in far]
    y_first, y_second = far, [b for _, b in from_far]
    got_x = lax.ppermute(e1, "cols", [pair for pair in first if pair not in to_late])
    got_up = along_rows(up, -1)
    got_dn = along_rows(dn, 1)
    got_z = lax.ppermute(e2, "cols", [pair for pair in second if pair not in from_far])
    p_early, again = call(
        project_early_kernel,
        [arr(2, 512, 3 * INNER), arr(144, D)],
        [up, dn, e1, e2, fixed(qkv_weight)],
        1_000,
        held=(4,),
        scratch=[pltpu.VMEM((D, 3 * INNER), BF), pltpu.SemaphoreType.DMA((3,))],
    )
    got_y = lax.ppermute(again, "cols", to_late + from_far)
    p_late = call(project_late_kernel, [arr(2, 512, 3 * INNER)], [up, dn, qkv_weight], 1_000)
    inner, kve = call(
        inner_kernel,
        [arr(2, 3, 128, INNER), arr(2, 2, 64, 2 * INNER)],
        [got_up, got_dn, p_early, p_late, qkv_weight, orders],
        1_000,
    )
    to_up, to_dn = call(merge_kernel, [arr(128, D), arr(160, D)], [got_x, got_z, kve], 1_000, anywhere=(2,))
    ux = along_rows(to_up, -1)
    dx = along_rows(to_dn, 1)
    far_up, far_dn = call(split_kernel, [arr(64, D), arr(80, D)], [got_y, to_up], STRIP_FLOPS, anywhere=(1,))
    uy = along_rows(far_up, -1)
    dy = along_rows(far_dn, 1)
    kvf = call(
        functools.partial(strips_kernel, y_first, y_second),
        [arr(2, 2, 64, 2 * INNER)],
        [got_x, got_y, got_z, qkv_weight, far_up],
        1_000,
        anywhere=(4,),
    )
    return call(
        functools.partial(edge_kernel, y_first, y_second),
        [arr(16, 64, INNER)],
        [ux, uy, dx, dy, got_x, got_y, got_z, kvf, qkv_weight, orders, got_dn, p_early, p_late, inner, kve],
        1_000,
        scratch=[pltpu.VMEM((2, 2, 64, INNER), F32)],
    )


def solution(mesh):
    in_specs = (P(("batch", "rows"), "cols", None), P(), P(("batch", "rows"), "cols", None))
    out_specs = P(("batch", "rows"), "cols", None)
    return jax.shard_map(
        per_device, mesh=mesh, in_specs=in_specs, out_specs=out_specs, check_vma=False
    )
```

```python
import functools

import jax
import jax.numpy as jnp
from jax import lax
from jax.experimental import pallas as pl
from jax.experimental.pallas import tpu as pltpu
from jax.sharding import PartitionSpec as P

D = 1024
HEADS = 8
HEAD_DIM = 64
INNER = 512
HALF = 8
EPSILON = 1e-06
LOG2E = 1.4426950408889634
FAR = 4096.0
BF = jnp.bfloat16
F32 = jnp.float32
MIB = 1 << 20


def normalize(values):
    center = jnp.mean(values, axis=-1, keepdims=True)
    off = values - center
    spread = jnp.mean(off * off, axis=-1, keepdims=True)
    return off * lax.rsqrt(spread + EPSILON)


def put_tokens(ref, per, at, values):
    for k in range(8):
        ref[per * k + at : per * k + at + values.shape[0], :] = values[:, 128 * k : 128 * k + 128]


def get_tokens(ref, per, at, count):
    return jnp.concatenate([ref[per * k + at : per * k + at + count, :] for k in range(8)], axis=1)


def get_ranks(block):
    block = block.astype(F32)
    return jnp.concatenate([block[0:1], block[8:9]], axis=1)


def store_ranks(ord_ref, dn, strips):
    ranks = ord_ref[0].astype(F32).astype(BF)
    natural = lax.broadcasted_iota(jnp.int32, (256, 256), 0)
    m = lax.broadcasted_iota(jnp.int32, (256, 256), 1)
    source = ((m >> 7) * 8 + ((m >> 3) & 7)) * 16 + ((m >> 6) & 1) * 8 + (m & 7)
    quads = jnp.dot(ranks, (natural == source).astype(F32).astype(BF), preferred_element_type=F32)
    rank_row = jnp.concatenate(
        [ranks[0:1].astype(F32), ranks[1:2].astype(F32), ranks[2:3].astype(F32), quads[3:4]], axis=1
    )
    dn[512:528, :] = jnp.broadcast_to(rank_row, (16, D)).astype(BF)
    halves = [jnp.broadcast_to(quads[3:4, 128 * n : 128 * n + 128], (8, 128)) for n in range(2)]
    for ref in strips:
        ref[1024:1040, :] = jnp.concatenate(halves, axis=0).astype(BF)


def put_strips(odd, at, left, right, e1, e2):
    put_tokens(e1, 128, at, jnp.where(odd, right, left))
    put_tokens(e2, 128, at, jnp.where(odd, left, right))


def pack_rows(x_ref, ord_hbm, up, dn, held, ord_ref, sem, strips=()):
    odd = lax.rem(lax.axis_index("cols"), 2) == 1
    copies = [
        pltpu.make_async_copy(x_ref.at[pl.ds(4 * q, 4)], held.at[pl.ds(4 * q, 4)], sem.at[q]) for q in range(4)
    ]
    ranks_copy = pltpu.make_async_copy(ord_hbm, ord_ref, sem.at[4])
    ranks_copy.start()
    for copy in copies:
        copy.start()
    ranks_copy.wait()
    store_ranks(ord_ref, dn, strips)
    for q in range(8):
        if q % 2 == 0:
            copies[q // 2].wait()
        h, t = q // 4, q % 4
        ref = dn if h else up
        lefts, rights = [], []
        for u in range(2):
            before = None
            for k in range(4):
                part = normalize(held[2 * q + u, 16 * k : 16 * k + 16, :].astype(F32))
                if k == 0:
                    lefts.append(part[:8])
                else:
                    at = 128 * (k - 1) + (2 * t + u) * 16
                    ref[at : at + 16, :] = jnp.concatenate([before, part[:8]], axis=0).astype(BF)
                before = part[8:]
            rights.append(before)
        left = jnp.concatenate(lefts, axis=0).astype(BF)
        right = jnp.concatenate(rights, axis=0).astype(BF)
        ref[384 + t * 16 : 400 + t * 16, :] = left
        ref[448 + t * 16 : 464 + t * 16, :] = right
        put_strips(odd, 64 * h + t * 16, left, right, *strips)


def pack_kernel(x_ref, ord_hbm, up, dn, e1, e2, held, ord_ref, sem):
    pack_rows(x_ref, ord_hbm, up, dn, held, ord_ref, sem, (e1, e2))


def is_early():
    return lax.axis_index("cols") < lax.axis_size("cols") // 2


def project_early_kernel(up, dn, e1, w_hbm, p, e1_again, w_ref, sem):
    @pl.when(is_early())
    def _():
        e1_again[...] = e1[...]
        copies = []
        for n in range(3):
            at = pl.ds(INNER * n, INNER)
            copies.append(pltpu.make_async_copy(w_hbm.at[:, at], w_ref.at[:, at], sem.at[n]))
        for copy in copies:
            copy.start()
        for n, copy in enumerate(copies):
            copy.wait()
            at = slice(INNER * n, INNER * n + INNER)
            for h, src in enumerate((up, dn)):
                p[h, :, at] = jnp.dot(src[0:512, :], w_ref[:, at], preferred_element_type=F32).astype(BF)


def hold_kernel(value, tie, same):
    del tie
    same[...] = value[...]


def project_late_kernel(up, dn, w_ref, tie, p):
    del tie

    @pl.when(jnp.logical_not(is_early()))
    def _():
        for h, src in enumerate((up, dn)):
            for q in range(2):
                at = slice(256 * q, 256 * q + 256)
                p[h, at, :] = jnp.dot(src[at, :], w_ref[...], preferred_element_type=F32).astype(BF)


def column_of(row, count):
    q = lax.broadcasted_iota(jnp.int32, (count, 128), 0)
    lane = lax.broadcasted_iota(jnp.int32, (count, 128), 1)
    return jnp.sum(jnp.where(q == lane, jnp.broadcast_to(row, (count, 128)), 0.0), axis=1, keepdims=True)


def attend(query, keys, values, allowed):
    count = query.shape[0]
    both = jnp.concatenate([allowed, allowed], axis=0)
    first = lax.broadcasted_iota(jnp.int32, (count, 128), 1) < HEAD_DIM
    ones = jnp.ones((256, 128), BF)
    outs = []
    for g in range(4):
        at = slice(128 * g, 128 * g + 128)
        q = query[:, at]
        zero = jnp.zeros_like(q)
        q = jnp.concatenate([jnp.where(first, q, zero), jnp.where(first, zero, q)], axis=0)
        s = lax.dot_general(q, keys[:, at], (((1,), (1,)), ((), ())), preferred_element_type=F32)
        s = jnp.where(both, s, -jnp.inf)
        top = jnp.max(s, axis=-1, keepdims=True)
        p = jnp.exp2((s - top) * (LOG2E * HEAD_DIM**-0.5)).astype(BF)
        o = jnp.dot(p, jnp.concatenate([values[:, at], ones], axis=1), preferred_element_type=F32)
        number = jnp.where(first, o[:count, :128], o[count:, :128])
        total = jnp.where(first, o[:count, 128:], o[count:, 128:])
        outs.append(number / total)
    return jnp.concatenate(outs, axis=1)


def inner_window(h, j, own, other_kv, rank_row, last, out):
    own_ranks = rank_row[:, 128:] if h == 0 else rank_row[:, :128]
    other_ranks = (rank_row[:, :128] if h == 0 else rank_row[:, 128:]) + jnp.where(last, FAR, 0.0)
    key_ranks = jnp.concatenate([own_ranks, other_ranks], axis=1)
    allowed = key_ranks <= column_of(own_ranks, 128)
    keys = jnp.concatenate([own[:, INNER : 2 * INNER], other_kv[:, :INNER]], axis=0)
    values = jnp.concatenate([own[:, 2 * INNER :], other_kv[:, INNER:]], axis=0)
    out[h, j] = attend(own[:, :INNER], keys, values, allowed).astype(BF)


def last_pair(h):
    size = lax.axis_size("rows")
    return lax.axis_index("rows") == (0 if h == 0 else size - 1)


def by_side(body, p_early, p_late):
    early = is_early()
    pl.when(early)(lambda: body(p_early))
    pl.when(jnp.logical_not(early))(lambda: body(p_late))


def inner_kernel(up, dn, p_early, p_late, w_ref, ord_ref, out, kve):
    by_side(lambda p: inner_windows(up, dn, p, w_ref, ord_ref, out, kve), p_early, p_late)


def inner_windows(up, dn, p, w_ref, ord_ref, out, kve):
    for h, src in enumerate((dn, up)):
        kv = jnp.dot(src[0:512, :], w_ref[:, INNER:], preferred_element_type=F32).astype(BF)
        for j in range(3):
            if h == 0:
                ranks = dn[512:528, 256 * j : 256 * j + 256].astype(F32)[0:1]
            else:
                ranks = ord_ref[0, j : j + 1, :].astype(F32)
            at = slice(128 * j, 128 * j + 128)
            inner_window(h, j, p[h, at, :], kv[at], ranks, last_pair(h), out)
        kve[h, 0] = kv[384:448]
        kve[h, 1] = kv[448:512]


def one_of(cols):
    col = lax.axis_index("cols")
    return functools.reduce(jnp.logical_or, [col == c for c in cols])


def choose_kernel(far, got_x, got_y, e1):
    e1[...] = jnp.where(one_of(far), got_y[...], got_x[...])


def merge_kernel(first, second, to_up, to_dn):
    for e, src in enumerate((first, second)):
        put_tokens(to_up, 128, 64 * e, get_tokens(src, 128, 0, 64))
        put_tokens(to_dn, 128, 64 * e, get_tokens(src, 128, 64, 64))
        to_dn[1024 + 16 * e : 1040 + 16 * e, :] = src[1024:1040, :]


def strips_kernel(first, second, w_ref, tie, kvf):
    del tie
    for e, src in enumerate((first, second)):
        kv = jnp.dot(get_tokens(src, 128, 0, 128), w_ref[:, INNER:], preferred_element_type=F32).astype(BF)
        kvf[e, 0] = kv[0:64]
        kvf[e, 1] = kv[64:128]


def edge_kernel(up, down, first, second, kvf, w_ref, own_strip, dn, p_early, p_late, inner, kve, out_hbm, edge, out, sem):
    ups = [get_tokens(up, 128, 64 * e, 64) for e in range(2)]
    downs = [get_tokens(down, 128, 64 * e, 64) for e in range(2)]
    corners = [get_ranks(down[1024 + 16 * e : 1040 + 16 * e, :]) for e in range(2)]
    besides = [get_ranks(src[1024:1040, :]) for src in (first, second)]
    diags = jnp.concatenate(downs + ups, axis=0)
    kvd = jnp.dot(diags, w_ref[:, INNER:], preferred_element_type=F32).astype(BF)
    mine = get_ranks(own_strip[1024:1040, :])
    copies = [pltpu.make_async_copy(out.at[pl.ds(8 * h, 8)], out_hbm.at[pl.ds(8 * h, 8)], sem.at[h]) for h in range(2)]
    col = lax.axis_index("cols")
    odd = lax.rem(col, 2)

    def edges(p):
        above = dn[512:528, 768:1024].astype(F32)[0:1]
        lane = lax.broadcasted_iota(jnp.int32, (1, 128), 1)
        for h in range(2):
            for e, (beside, corner) in enumerate(zip(besides, corners)):
                side = odd if e == 0 else 1 - odd
                is_left = side == 0
                last_col = jnp.where(is_left, col == 0, col == lax.axis_size("cols") - 1)
                ranks = jnp.where(is_left, corner, above) if h == 0 else jnp.where(is_left, beside, mine)
                half_own = ranks[:, 128:] if h == 0 else ranks[:, :128]
                half_other = ranks[:, :128] if h == 0 else ranks[:, 128:]
                half_own, half_other = (
                    jnp.where(is_left, jnp.concatenate([x[:, 64:], x[:, :64]], axis=1), x) for x in (half_own, half_other)
                )
                far_col = jnp.where((lane >= 64) & last_col, FAR, 0.0)
                key_ranks = jnp.concatenate(
                    [half_own + far_col, half_other + far_col + jnp.where(last_pair(h), FAR, 0.0)], axis=1
                )
                allowed = key_ranks <= column_of(half_own, 64)
                own = p[h, pl.ds(pl.multiple_of(384 + 64 * side, 64), 64), :]
                near = kve[h, side]
                far = kvf[e, h]
                cross = kvd[128 * h + 64 * e : 128 * h + 64 * e + 64]
                keys = jnp.concatenate(
                    [own[:, INNER : 2 * INNER], far[:, :INNER], near[:, :INNER], cross[:, :INNER]], axis=0
                )
                values = jnp.concatenate([own[:, 2 * INNER :], far[:, INNER:], near[:, INNER:], cross[:, INNER:]], axis=0)
                edge[side] = attend(own[:, :INNER], keys, values, allowed)
            for i in range(HALF):
                row = [edge[0, 8 * i : 8 * i + 8]]
                row += [inner[h, j, 16 * i : 16 * i + 16].astype(F32) for j in range(3)]
                row += [edge[1, 8 * i : 8 * i + 8]]
                out[h * HALF + i] = jnp.concatenate(row, axis=0).astype(BF)
            copies[h].start()
        for copy in copies:
            copy.wait()

    by_side(edges, p_early, p_late)


STRIP_FLOPS = 1000
MERGE_FLOPS = 1_000_000_000
VMEM = pl.BlockSpec(memory_space=pltpu.VMEM)
ANY = pl.BlockSpec(memory_space=pl.ANY)
HBM = pl.BlockSpec(memory_space=pltpu.HBM)


def call(kernel, outs, args, flops, anywhere=(), scratch=(), aliases=None, limit=24, held=(), to_hbm=False):
    single = len(outs) == 1
    return pl.pallas_call(
        kernel,
        out_shape=outs[0] if single else tuple(outs),
        in_specs=[HBM if i in held else ANY if i in anywhere else VMEM for i in range(len(args))],
        out_specs=HBM if to_hbm else VMEM if single else tuple([VMEM] * len(outs)),
        scratch_shapes=list(scratch),
        input_output_aliases=aliases or {},
        compiler_params=pltpu.CompilerParams(vmem_limit_bytes=limit * MIB),
        cost_estimate=pl.CostEstimate(flops=flops, bytes_accessed=1_000, transcendentals=0),
    )(*args)


def arr(*shape):
    return jax.ShapeDtypeStruct(shape, BF)


def along_rows(value, by):
    size = lax.axis_size("rows")
    return lax.ppermute(value, "rows", [(i, (i + by) % size) for i in range(size)])


def fixed(x):
    return pltpu.with_memory_space_constraint(x, pltpu.HBM)


def per_device(features, qkv_weight, orders):
    cols = lax.axis_size("cols")
    half = cols // 2
    up, dn, e1, e2 = call(
        pack_kernel,
        [arr(512, D), arr(528, D), arr(1040, 128), arr(1040, 128)],
        [fixed(features), fixed(orders)],
        1_000,
        held=(0, 1),
        scratch=[pltpu.VMEM((16, 64, D), BF), pltpu.VMEM((1, 4, 256), jnp.int32), pltpu.SemaphoreType.DMA((5,))],
        limit=16,
    )
    first = [(c, (c + 1) % cols if c % 2 else (c - 1) % cols) for c in range(cols)]
    second = [(c, (c - 1) % cols if c % 2 else (c + 1) % cols) for c in range(cols)]
    to_late = [(a, b) for a, b in first if a < half <= b]
    far = [b for _, b in to_late]
    got_x = lax.ppermute(e1, "cols", [pair for pair in first if pair not in to_late])
    got_up = along_rows(up, -1)
    got_dn = along_rows(dn, 1)
    p_early, again = call(
        project_early_kernel,
        [arr(2, 512, 3 * INNER), arr(1040, 128)],
        [up, dn, e1, fixed(qkv_weight)],
        1_000,
        held=(3,),
        scratch=[pltpu.VMEM((D, 3 * INNER), BF), pltpu.SemaphoreType.DMA((3,))],
    )
    got_y = lax.ppermute(again, "cols", to_late)
    p_late = call(
        project_late_kernel, [arr(2, 512, 3 * INNER)], [up, dn, qkv_weight, again], 1_000, anywhere=(3,)
    )
    e2_again = call(hold_kernel, [arr(1040, 128)], [e2, p_late], 1_000, anywhere=(1,))
    got_z = lax.ppermute(e2_again, "cols", second)
    inner, kve = call(
        inner_kernel,
        [arr(2, 3, 128, INNER), arr(2, 2, 64, 2 * INNER)],
        [got_up, got_dn, p_early, p_late, qkv_weight, orders],
        1_000,
    )
    got_x = call(hold_kernel, [arr(1040, 128)], [got_x, kve], MERGE_FLOPS, anywhere=(1,))
    got_e1 = call(functools.partial(choose_kernel, far), [arr(1040, 128)], [got_x, got_y], MERGE_FLOPS)
    to_up, to_dn = call(merge_kernel, [arr(1024, 128), arr(1056, 128)], [got_e1, got_z], 1_000)
    hop_up = along_rows(to_up, -1)
    hop_dn = along_rows(to_dn, 1)
    kvf = call(
        strips_kernel, [arr(2, 2, 64, 2 * INNER)], [got_e1, got_z, qkv_weight, to_up], STRIP_FLOPS, anywhere=(3,)
    )
    return call(
        edge_kernel,
        [arr(16, 64, INNER)],
        [hop_up, hop_dn, got_e1, got_z, kvf, qkv_weight, e1, got_dn, p_early, p_late, inner, kve],
        1_000,
        scratch=[pltpu.VMEM((2, 64, INNER), F32), pltpu.VMEM((16, 64, INNER), BF), pltpu.SemaphoreType.DMA((2,))],
        to_hbm=True,
    )


def solution(mesh):
    in_specs = (P(("batch", "rows"), "cols", None), P(), P(("batch", "rows"), "cols", None))
    out_specs = P(("batch", "rows"), "cols", None)
    return jax.shard_map(
        per_device, mesh=mesh, in_specs=in_specs, out_specs=out_specs, check_vma=False
    )
```

```python
import functools

import jax
import jax.numpy as jnp
from jax import lax
from jax.experimental import pallas as pl
from jax.experimental.pallas import tpu as pltpu
from jax.sharding import PartitionSpec as P

D = 1024
HEADS = 8
HEAD_DIM = 64
INNER = 512
HALF = 8
EPSILON = 1e-06
LOG2E = 1.4426950408889634
FAR = 4096.0
BF = jnp.bfloat16
F32 = jnp.float32
MIB = 1 << 20


def normalize(values):
    center = jnp.mean(values, axis=-1, keepdims=True)
    off = values - center
    spread = jnp.mean(off * off, axis=-1, keepdims=True)
    return off * lax.rsqrt(spread + EPSILON)


def put_tokens(ref, per, at, values):
    for k in range(8):
        ref[per * k + at : per * k + at + values.shape[0], :] = values[:, 128 * k : 128 * k + 128]


def get_tokens(ref, per, at, count):
    return jnp.concatenate([ref[per * k + at : per * k + at + count, :] for k in range(8)], axis=1)


def get_ranks(block):
    block = block.astype(F32)
    return jnp.concatenate([block[0:1], block[8:9]], axis=1)


def store_ranks(ord_ref, dn, strips):
    ranks = ord_ref[0].astype(F32).astype(BF)
    natural = lax.broadcasted_iota(jnp.int32, (256, 256), 0)
    m = lax.broadcasted_iota(jnp.int32, (256, 256), 1)
    source = ((m >> 7) * 8 + ((m >> 3) & 7)) * 16 + ((m >> 6) & 1) * 8 + (m & 7)
    quads = jnp.dot(ranks, (natural == source).astype(F32).astype(BF), preferred_element_type=F32)
    rank_row = jnp.concatenate(
        [ranks[0:1].astype(F32), ranks[1:2].astype(F32), ranks[2:3].astype(F32), quads[3:4]], axis=1
    )
    dn[512:528, :] = jnp.broadcast_to(rank_row, (16, D)).astype(BF)
    halves = [jnp.broadcast_to(quads[3:4, 128 * n : 128 * n + 128], (8, 128)) for n in range(2)]
    for ref in strips:
        ref[1024:1040, :] = jnp.concatenate(halves, axis=0).astype(BF)


def put_strips(odd, at, left, right, e1, e2):
    put_tokens(e1, 128, at, jnp.where(odd, right, left))
    put_tokens(e2, 128, at, jnp.where(odd, left, right))


def pack_rows(x_ref, ord_hbm, up, dn, held, ord_ref, sem, strips=()):
    odd = lax.rem(lax.axis_index("cols"), 2) == 1
    copies = [
        pltpu.make_async_copy(x_ref.at[pl.ds(4 * q, 4)], held.at[pl.ds(4 * q, 4)], sem.at[q]) for q in range(4)
    ]
    ranks_copy = pltpu.make_async_copy(ord_hbm, ord_ref, sem.at[4])
    ranks_copy.start()
    for copy in copies:
        copy.start()
    ranks_copy.wait()
    store_ranks(ord_ref, dn, strips)
    for q in range(8):
        if q % 2 == 0:
            copies[q // 2].wait()
        h, t = q // 4, q % 4
        ref = dn if h else up
        lefts, rights = [], []
        for u in range(2):
            before = None
            for k in range(4):
                part = normalize(held[2 * q + u, 16 * k : 16 * k + 16, :].astype(F32))
                if k == 0:
                    lefts.append(part[:8])
                else:
                    at = 128 * (k - 1) + (2 * t + u) * 16
                    ref[at : at + 16, :] = jnp.concatenate([before, part[:8]], axis=0).astype(BF)
                before = part[8:]
            rights.append(before)
        left = jnp.concatenate(lefts, axis=0).astype(BF)
        right = jnp.concatenate(rights, axis=0).astype(BF)
        ref[384 + t * 16 : 400 + t * 16, :] = left
        ref[448 + t * 16 : 464 + t * 16, :] = right
        put_strips(odd, 64 * h + t * 16, left, right, *strips)


def pack_kernel(x_ref, ord_hbm, up, dn, e1, e2, held, ord_ref, sem):
    pack_rows(x_ref, ord_hbm, up, dn, held, ord_ref, sem, (e1, e2))


def is_early():
    return lax.axis_index("cols") < lax.axis_size("cols") // 2


def project_early_kernel(up, dn, e1, w_hbm, p, e1_again, w_ref, sem):
    @pl.when(is_early())
    def _():
        e1_again[...] = e1[...]
        copies = []
        for n in range(3):
            at = pl.ds(INNER * n, INNER)
            copies.append(pltpu.make_async_copy(w_hbm.at[:, at], w_ref.at[:, at], sem.at[n]))
        for copy in copies:
            copy.start()
        for n, copy in enumerate(copies):
            copy.wait()
            at = slice(INNER * n, INNER * n + INNER)
            for h, src in enumerate((up, dn)):
                p[h, :, at] = jnp.dot(src[0:512, :], w_ref[:, at], preferred_element_type=F32).astype(BF)


def hold_kernel(value, tie, same):
    del tie
    same[...] = value[...]


def project_late_kernel(up, dn, w_ref, tie, p):
    del tie

    @pl.when(jnp.logical_not(is_early()))
    def _():
        for h, src in enumerate((up, dn)):
            for q in range(2):
                at = slice(256 * q, 256 * q + 256)
                p[h, at, :] = jnp.dot(src[at, :], w_ref[...], preferred_element_type=F32).astype(BF)


def column_of(row, count):
    q = lax.broadcasted_iota(jnp.int32, (count, 128), 0)
    lane = lax.broadcasted_iota(jnp.int32, (count, 128), 1)
    return jnp.sum(jnp.where(q == lane, jnp.broadcast_to(row, (count, 128)), 0.0), axis=1, keepdims=True)


def attend(query, keys, values, allowed):
    count = query.shape[0]
    both = jnp.concatenate([allowed, allowed], axis=0)
    first = lax.broadcasted_iota(jnp.int32, (count, 128), 1) < HEAD_DIM
    ones = jnp.ones((256, 128), BF)
    outs = []
    for g in range(4):
        at = slice(128 * g, 128 * g + 128)
        q = query[:, at]
        zero = jnp.zeros_like(q)
        q = jnp.concatenate([jnp.where(first, q, zero), jnp.where(first, zero, q)], axis=0)
        s = lax.dot_general(q, keys[:, at], (((1,), (1,)), ((), ())), preferred_element_type=F32)
        s = jnp.where(both, s, -jnp.inf)
        top = jnp.max(s, axis=-1, keepdims=True)
        p = jnp.exp2((s - top) * (LOG2E * HEAD_DIM**-0.5)).astype(BF)
        o = jnp.dot(p, jnp.concatenate([values[:, at], ones], axis=1), preferred_element_type=F32)
        number = jnp.where(first, o[:count, :128], o[count:, :128])
        total = jnp.where(first, o[:count, 128:], o[count:, 128:])
        outs.append(number / total)
    return jnp.concatenate(outs, axis=1)


def inner_window(h, j, own, other_kv, rank_row, last, out):
    own_ranks = rank_row[:, 128:] if h == 0 else rank_row[:, :128]
    other_ranks = (rank_row[:, :128] if h == 0 else rank_row[:, 128:]) + jnp.where(last, FAR, 0.0)
    key_ranks = jnp.concatenate([own_ranks, other_ranks], axis=1)
    allowed = key_ranks <= column_of(own_ranks, 128)
    keys = jnp.concatenate([own[:, INNER : 2 * INNER], other_kv[:, :INNER]], axis=0)
    values = jnp.concatenate([own[:, 2 * INNER :], other_kv[:, INNER:]], axis=0)
    out[h, j] = attend(own[:, :INNER], keys, values, allowed).astype(BF)


def last_pair(h):
    size = lax.axis_size("rows")
    return lax.axis_index("rows") == (0 if h == 0 else size - 1)


def by_side(body, p_early, p_late):
    early = is_early()
    pl.when(early)(lambda: body(p_early))
    pl.when(jnp.logical_not(early))(lambda: body(p_late))


def inner_kernel(up, dn, p_early, p_late, w_ref, ord_ref, tie, out, kve):
    del tie
    by_side(lambda p: inner_windows(up, dn, p, w_ref, ord_ref, out, kve), p_early, p_late)


def inner_windows(up, dn, p, w_ref, ord_ref, out, kve):
    for h, src in enumerate((dn, up)):
        kv = jnp.dot(src[0:512, :], w_ref[:, INNER:], preferred_element_type=F32).astype(BF)
        for j in range(3):
            if h == 0:
                ranks = dn[512:528, 256 * j : 256 * j + 256].astype(F32)[0:1]
            else:
                ranks = ord_ref[0, j : j + 1, :].astype(F32)
            at = slice(128 * j, 128 * j + 128)
            inner_window(h, j, p[h, at, :], kv[at], ranks, last_pair(h), out)
        kve[h, 0] = kv[384:448]
        kve[h, 1] = kv[448:512]


def one_of(cols):
    col = lax.axis_index("cols")
    return functools.reduce(jnp.logical_or, [col == c for c in cols])


def choose_kernel(far, got_x, got_y, e1):
    e1[...] = jnp.where(one_of(far), got_y[...], got_x[...])


def split_kernel(strip, to_up, to_dn):
    put_tokens(to_up, 64, 0, get_tokens(strip, 128, 0, 64))
    put_tokens(to_dn, 64, 0, get_tokens(strip, 128, 64, 64))
    to_dn[512:528, :] = strip[1024:1040, :]


def gather_kernel(e2, got_up, got_dn, z):
    odd = lax.rem(lax.axis_index("cols"), 2)
    at = pl.ds(pl.multiple_of(384 + 64 * (1 - odd), 64), 64)
    put_tokens(z, 256, 0, get_tokens(e2, 128, 0, 128))
    put_tokens(z, 256, 128, got_dn[at, :])
    put_tokens(z, 256, 192, got_up[at, :])
    z[2048:2064, :] = e2[1024:1040, :]
    ranks = got_dn[512:528, 768:1024].astype(F32)
    z[2064:2080, :] = jnp.concatenate([ranks[0:8, :128], ranks[8:16, 128:]], axis=0).astype(BF)


def strips_kernel(first, second, w_ref, tie, kvf, kvz):
    del tie
    tokens = jnp.concatenate([get_tokens(first, 128, 0, 128), get_tokens(second, 256, 0, 256)], axis=0)
    kv = jnp.dot(tokens, w_ref[:, INNER:], preferred_element_type=F32).astype(BF)
    for n in range(2):
        for e in range(2):
            kvf[e, n] = kv[128 * e + 64 * n : 128 * e + 64 * n + 64]
        kvz[n] = kv[256 + 64 * n : 320 + 64 * n]


def edge_kernel(
    up, down, first, second, kvf, kvz, w_ref, own_strip, dn, p_early, p_late, inner, kve, out_hbm, edge, out, sem
):
    diags = jnp.concatenate([get_tokens(down, 64, 0, 64), get_tokens(up, 64, 0, 64)], axis=0)
    kvd = jnp.dot(diags, w_ref[:, INNER:], preferred_element_type=F32).astype(BF)
    corners = [get_ranks(down[512:528, :]), get_ranks(second[2064:2080, :])]
    besides = [get_ranks(first[1024:1040, :]), get_ranks(second[2048:2064, :])]
    mine = get_ranks(own_strip[1024:1040, :])
    copies = [pltpu.make_async_copy(out.at[pl.ds(8 * h, 8)], out_hbm.at[pl.ds(8 * h, 8)], sem.at[h]) for h in range(2)]
    col = lax.axis_index("cols")
    odd = lax.rem(col, 2)

    def edges(p):
        above = dn[512:528, 768:1024].astype(F32)[0:1]
        lane = lax.broadcasted_iota(jnp.int32, (1, 128), 1)
        for h in range(2):
            for e, (beside, corner) in enumerate(zip(besides, corners)):
                side = odd if e == 0 else 1 - odd
                is_left = side == 0
                last_col = jnp.where(is_left, col == 0, col == lax.axis_size("cols") - 1)
                ranks = jnp.where(is_left, corner, above) if h == 0 else jnp.where(is_left, beside, mine)
                half_own = ranks[:, 128:] if h == 0 else ranks[:, :128]
                half_other = ranks[:, :128] if h == 0 else ranks[:, 128:]
                half_own, half_other = (
                    jnp.where(is_left, jnp.concatenate([x[:, 64:], x[:, :64]], axis=1), x) for x in (half_own, half_other)
                )
                far_col = jnp.where((lane >= 64) & last_col, FAR, 0.0)
                key_ranks = jnp.concatenate(
                    [half_own + far_col, half_other + far_col + jnp.where(last_pair(h), FAR, 0.0)], axis=1
                )
                allowed = key_ranks <= column_of(half_own, 64)
                own = p[h, pl.ds(pl.multiple_of(384 + 64 * side, 64), 64), :]
                near = kve[h, side]
                far = kvf[e, h]
                cross = kvz[h] if e else kvd[64 * h : 64 * h + 64]
                keys = jnp.concatenate(
                    [own[:, INNER : 2 * INNER], far[:, :INNER], near[:, :INNER], cross[:, :INNER]], axis=0
                )
                values = jnp.concatenate([own[:, 2 * INNER :], far[:, INNER:], near[:, INNER:], cross[:, INNER:]], axis=0)
                edge[side] = attend(own[:, :INNER], keys, values, allowed)
            for i in range(HALF):
                row = [edge[0, 8 * i : 8 * i + 8]]
                row += [inner[h, j, 16 * i : 16 * i + 16].astype(F32) for j in range(3)]
                row += [edge[1, 8 * i : 8 * i + 8]]
                out[h * HALF + i] = jnp.concatenate(row, axis=0).astype(BF)
            copies[h].start()
        for copy in copies:
            copy.wait()

    by_side(edges, p_early, p_late)


SPLIT_FLOPS = 10000000000
VMEM = pl.BlockSpec(memory_space=pltpu.VMEM)
ANY = pl.BlockSpec(memory_space=pl.ANY)
HBM = pl.BlockSpec(memory_space=pltpu.HBM)


def call(kernel, outs, args, flops, anywhere=(), scratch=(), aliases=None, limit=24, held=(), to_hbm=False):
    single = len(outs) == 1
    return pl.pallas_call(
        kernel,
        out_shape=outs[0] if single else tuple(outs),
        in_specs=[HBM if i in held else ANY if i in anywhere else VMEM for i in range(len(args))],
        out_specs=HBM if to_hbm else VMEM if single else tuple([VMEM] * len(outs)),
        scratch_shapes=list(scratch),
        input_output_aliases=aliases or {},
        compiler_params=pltpu.CompilerParams(vmem_limit_bytes=limit * MIB),
        cost_estimate=pl.CostEstimate(flops=flops, bytes_accessed=1_000, transcendentals=0),
    )(*args)


def arr(*shape):
    return jax.ShapeDtypeStruct(shape, BF)


def along_rows(value, by):
    size = lax.axis_size("rows")
    return lax.ppermute(value, "rows", [(i, (i + by) % size) for i in range(size)])


def fixed(x):
    return pltpu.with_memory_space_constraint(x, pltpu.HBM)


def per_device(features, qkv_weight, orders):
    cols = lax.axis_size("cols")
    half = cols // 2
    up, dn, e1, e2 = call(
        pack_kernel,
        [arr(512, D), arr(528, D), arr(1040, 128), arr(1040, 128)],
        [fixed(features), fixed(orders)],
        1_000,
        held=(0, 1),
        scratch=[pltpu.VMEM((16, 64, D), BF), pltpu.VMEM((1, 4, 256), jnp.int32), pltpu.SemaphoreType.DMA((5,))],
        limit=16,
    )
    first = [(c, (c + 1) % cols if c % 2 else (c - 1) % cols) for c in range(cols)]
    second = [(c, (c - 1) % cols if c % 2 else (c + 1) % cols) for c in range(cols)]
    to_late = [(a, b) for a, b in first if a < half <= b]
    far = [b for _, b in to_late]
    got_x = lax.ppermute(e1, "cols", [pair for pair in first if pair not in to_late])
    got_up = along_rows(up, -1)
    got_dn = along_rows(dn, 1)
    p_early, again = call(
        project_early_kernel,
        [arr(2, 512, 3 * INNER), arr(1040, 128)],
        [up, dn, e1, fixed(qkv_weight)],
        1_000,
        held=(3,),
        scratch=[pltpu.VMEM((D, 3 * INNER), BF), pltpu.SemaphoreType.DMA((3,))],
    )
    got_y = lax.ppermute(again, "cols", to_late)
    p_late = call(
        project_late_kernel, [arr(2, 512, 3 * INNER)], [up, dn, qkv_weight, again], 1_000, anywhere=(3,)
    )
    z = call(gather_kernel, [arr(2080, 128)], [e2, got_up, got_dn], 1_000)
    got_z = lax.ppermute(z, "cols", second)
    inner, kve = call(
        inner_kernel,
        [arr(2, 3, 128, INNER), arr(2, 2, 64, 2 * INNER)],
        [got_up, got_dn, p_early, p_late, qkv_weight, orders, z],
        1_000,
        anywhere=(6,),
    )
    got_x = call(hold_kernel, [arr(1040, 128)], [got_x, kve], 1_000, anywhere=(1,))
    got_e1 = call(functools.partial(choose_kernel, far), [arr(1040, 128)], [got_x, got_y], 1_000)
    to_up, to_dn = call(split_kernel, [arr(512, 128), arr(528, 128)], [got_e1], SPLIT_FLOPS)
    hop_up = along_rows(to_up, -1)
    hop_dn = along_rows(to_dn, 1)
    kvf, kvz = call(
        strips_kernel,
        [arr(2, 2, 64, 2 * INNER), arr(2, 64, 2 * INNER)],
        [got_e1, got_z, qkv_weight, to_up],
        1_000,
        anywhere=(3,),
    )
    return call(
        edge_kernel,
        [arr(16, 64, INNER)],
        [hop_up, hop_dn, got_e1, got_z, kvf, kvz, qkv_weight, e1, got_dn, p_early, p_late, inner, kve],
        1_000,
        scratch=[pltpu.VMEM((2, 64, INNER), F32), pltpu.VMEM((16, 64, INNER), BF), pltpu.SemaphoreType.DMA((2,))],
        to_hbm=True,
    )


def solution(mesh):
    in_specs = (P(("batch", "rows"), "cols", None), P(), P(("batch", "rows"), "cols", None))
    out_specs = P(("batch", "rows"), "cols", None)
    return jax.shard_map(
        per_device, mesh=mesh, in_specs=in_specs, out_specs=out_specs, check_vma=False
    )
```

```python
import functools

import jax
import jax.numpy as jnp
from jax import lax
from jax.experimental import pallas as pl
from jax.experimental.pallas import tpu as pltpu
from jax.sharding import PartitionSpec as P

D = 1024
HEADS = 8
HEAD_DIM = 64
INNER = 512
HALF = 8
EPSILON = 1e-06
LOG2E = 1.4426950408889634
FAR = 4096.0
BF = jnp.bfloat16
F32 = jnp.float32
MIB = 1 << 20


def normalize(values):
    center = jnp.mean(values, axis=-1, keepdims=True)
    off = values - center
    spread = jnp.mean(off * off, axis=-1, keepdims=True)
    return off * lax.rsqrt(spread + EPSILON)


def put_tokens(ref, per, at, values):
    for k in range(8):
        ref[per * k + at : per * k + at + values.shape[0], :] = values[:, 128 * k : 128 * k + 128]


def get_tokens(ref, per, at, count):
    return jnp.concatenate([ref[per * k + at : per * k + at + count, :] for k in range(8)], axis=1)


def get_ranks(block):
    block = block.astype(F32)
    return jnp.concatenate([block[0:1], block[8:9]], axis=1)


def store_ranks(ord_ref, dn, strips):
    ranks = ord_ref[0].astype(F32).astype(BF)
    natural = lax.broadcasted_iota(jnp.int32, (256, 256), 0)
    m = lax.broadcasted_iota(jnp.int32, (256, 256), 1)
    source = ((m >> 7) * 8 + ((m >> 3) & 7)) * 16 + ((m >> 6) & 1) * 8 + (m & 7)
    quads = jnp.dot(ranks, (natural == source).astype(F32).astype(BF), preferred_element_type=F32)
    rank_row = jnp.concatenate(
        [ranks[0:1].astype(F32), ranks[1:2].astype(F32), ranks[2:3].astype(F32), quads[3:4]], axis=1
    )
    dn[512:528, :] = jnp.broadcast_to(rank_row, (16, D)).astype(BF)
    halves = [jnp.broadcast_to(quads[3:4, 128 * n : 128 * n + 128], (8, 128)) for n in range(2)]
    for ref in strips:
        ref[1024:1040, :] = jnp.concatenate(halves, axis=0).astype(BF)


def put_strips(odd, at, left, right, e1, e2):
    put_tokens(e1, 128, at, jnp.where(odd, right, left))
    put_tokens(e2, 128, at, jnp.where(odd, left, right))


def pack_rows(x_ref, ord_hbm, up, dn, held, ord_ref, sem, strips=()):
    odd = lax.rem(lax.axis_index("cols"), 2) == 1
    copies = [
        pltpu.make_async_copy(x_ref.at[pl.ds(4 * q, 4)], held.at[pl.ds(4 * q, 4)], sem.at[q]) for q in range(4)
    ]
    ranks_copy = pltpu.make_async_copy(ord_hbm, ord_ref, sem.at[4])
    ranks_copy.start()
    for copy in copies:
        copy.start()
    ranks_copy.wait()
    store_ranks(ord_ref, dn, strips)
    for q in range(8):
        if q % 2 == 0:
            copies[q // 2].wait()
        h, t = q // 4, q % 4
        ref = dn if h else up
        lefts, rights = [], []
        for u in range(2):
            before = None
            for k in range(4):
                part = normalize(held[2 * q + u, 16 * k : 16 * k + 16, :].astype(F32))
                if k == 0:
                    lefts.append(part[:8])
                else:
                    at = 128 * (k - 1) + (2 * t + u) * 16
                    ref[at : at + 16, :] = jnp.concatenate([before, part[:8]], axis=0).astype(BF)
                before = part[8:]
            rights.append(before)
        left = jnp.concatenate(lefts, axis=0).astype(BF)
        right = jnp.concatenate(rights, axis=0).astype(BF)
        ref[384 + t * 16 : 400 + t * 16, :] = left
        ref[448 + t * 16 : 464 + t * 16, :] = right
        put_strips(odd, 64 * h + t * 16, left, right, *strips)


def pack_kernel(x_ref, ord_hbm, up, dn, e1, e2, held, ord_ref, sem):
    pack_rows(x_ref, ord_hbm, up, dn, held, ord_ref, sem, (e1, e2))


def is_early():
    return lax.axis_index("cols") < lax.axis_size("cols") // 2


def project_early_kernel(up, dn, e1, w_hbm, p, e1_again, w_ref, sem):
    @pl.when(is_early())
    def _():
        e1_again[...] = e1[...]
        copies = []
        for n in range(3):
            at = pl.ds(INNER * n, INNER)
            copies.append(pltpu.make_async_copy(w_hbm.at[:, at], w_ref.at[:, at], sem.at[n]))
        for copy in copies:
            copy.start()
        for n, copy in enumerate(copies):
            copy.wait()
            at = slice(INNER * n, INNER * n + INNER)
            for h, src in enumerate((up, dn)):
                p[h, :, at] = jnp.dot(src[0:512, :], w_ref[:, at], preferred_element_type=F32).astype(BF)


def hold_kernel(value, tie, same):
    del tie
    same[...] = value[...]


def project_late_kernel(up, dn, w_ref, tie, p):
    del tie

    @pl.when(jnp.logical_not(is_early()))
    def _():
        for h, src in enumerate((up, dn)):
            for q in range(2):
                at = slice(256 * q, 256 * q + 256)
                p[h, at, :] = jnp.dot(src[at, :], w_ref[...], preferred_element_type=F32).astype(BF)


def column_of(row, count):
    q = lax.broadcasted_iota(jnp.int32, (count, 128), 0)
    lane = lax.broadcasted_iota(jnp.int32, (count, 128), 1)
    return jnp.sum(jnp.where(q == lane, jnp.broadcast_to(row, (count, 128)), 0.0), axis=1, keepdims=True)


def attend(query, keys, values, allowed):
    count = query.shape[0]
    both = jnp.concatenate([allowed, allowed], axis=0)
    first = lax.broadcasted_iota(jnp.int32, (count, 128), 1) < HEAD_DIM
    ones = jnp.ones((256, 128), BF)
    outs = []
    for g in range(4):
        at = slice(128 * g, 128 * g + 128)
        q = query[:, at]
        zero = jnp.zeros_like(q)
        q = jnp.concatenate([jnp.where(first, q, zero), jnp.where(first, zero, q)], axis=0)
        s = lax.dot_general(q, keys[:, at], (((1,), (1,)), ((), ())), preferred_element_type=F32)
        s = jnp.where(both, s, -jnp.inf)
        top = jnp.max(s, axis=-1, keepdims=True)
        p = jnp.exp2((s - top) * (LOG2E * HEAD_DIM**-0.5)).astype(BF)
        o = jnp.dot(p, jnp.concatenate([values[:, at], ones], axis=1), preferred_element_type=F32)
        number = jnp.where(first, o[:count, :128], o[count:, :128])
        total = jnp.where(first, o[:count, 128:], o[count:, 128:])
        outs.append(number / total)
    return jnp.concatenate(outs, axis=1)


def inner_window(h, j, own, other_kv, rank_row, last, out):
    own_ranks = rank_row[:, 128:] if h == 0 else rank_row[:, :128]
    other_ranks = (rank_row[:, :128] if h == 0 else rank_row[:, 128:]) + jnp.where(last, FAR, 0.0)
    key_ranks = jnp.concatenate([own_ranks, other_ranks], axis=1)
    allowed = key_ranks <= column_of(own_ranks, 128)
    keys = jnp.concatenate([own[:, INNER : 2 * INNER], other_kv[:, :INNER]], axis=0)
    values = jnp.concatenate([own[:, 2 * INNER :], other_kv[:, INNER:]], axis=0)
    out[h, j] = attend(own[:, :INNER], keys, values, allowed).astype(BF)


def last_pair(h):
    size = lax.axis_size("rows")
    return lax.axis_index("rows") == (0 if h == 0 else size - 1)


def by_side(body, p_early, p_late):
    early = is_early()
    pl.when(early)(lambda: body(p_early))
    pl.when(jnp.logical_not(early))(lambda: body(p_late))


def inner_kernel(up, dn, p_early, p_late, w_ref, ord_ref, tie, out, kve):
    del tie
    by_side(lambda p: inner_windows(up, dn, p, w_ref, ord_ref, out, kve), p_early, p_late)


def inner_windows(up, dn, p, w_ref, ord_ref, out, kve):
    for h, src in enumerate((dn, up)):
        kv = jnp.dot(src[0:512, :], w_ref[:, INNER:], preferred_element_type=F32).astype(BF)
        for j in range(3):
            if h == 0:
                ranks = dn[512:528, 256 * j : 256 * j + 256].astype(F32)[0:1]
            else:
                ranks = ord_ref[0, j : j + 1, :].astype(F32)
            at = slice(128 * j, 128 * j + 128)
            inner_window(h, j, p[h, at, :], kv[at], ranks, last_pair(h), out)
        kve[h, 0] = kv[384:448]
        kve[h, 1] = kv[448:512]


def one_of(cols):
    col = lax.axis_index("cols")
    return functools.reduce(jnp.logical_or, [col == c for c in cols])


def choose_kernel(far, got_x, got_y, e1):
    e1[...] = jnp.where(one_of(far), got_y[...], got_x[...])


def split_kernel(strip, to_up, to_dn):
    put_tokens(to_up, 64, 0, get_tokens(strip, 128, 0, 64))
    put_tokens(to_dn, 64, 0, get_tokens(strip, 128, 64, 64))
    to_dn[512:528, :] = strip[1024:1040, :]


def gather_kernel(e2, got_up, got_dn, z):
    odd = lax.rem(lax.axis_index("cols"), 2)
    at = pl.ds(pl.multiple_of(384 + 64 * (1 - odd), 64), 64)
    put_tokens(z, 256, 0, get_tokens(e2, 128, 0, 128))
    put_tokens(z, 256, 128, got_dn[at, :])
    put_tokens(z, 256, 192, got_up[at, :])
    z[2048:2064, :] = e2[1024:1040, :]
    ranks = got_dn[512:528, 768:1024].astype(F32)
    z[2064:2080, :] = jnp.concatenate([ranks[0:8, :128], ranks[8:16, 128:]], axis=0).astype(BF)


def edge_window(h, side, ranks, p, near, far, cross):
    col = lax.axis_index("cols")
    lane = lax.broadcasted_iota(jnp.int32, (1, 128), 1)
    is_left = side == 0
    last_col = jnp.where(is_left, col == 0, col == lax.axis_size("cols") - 1)
    half_own = ranks[:, 128:] if h == 0 else ranks[:, :128]
    half_other = ranks[:, :128] if h == 0 else ranks[:, 128:]
    half_own, half_other = (
        jnp.where(is_left, jnp.concatenate([x[:, 64:], x[:, :64]], axis=1), x) for x in (half_own, half_other)
    )
    far_col = jnp.where((lane >= 64) & last_col, FAR, 0.0)
    key_ranks = jnp.concatenate([half_own + far_col, half_other + far_col + jnp.where(last_pair(h), FAR, 0.0)], axis=1)
    allowed = key_ranks <= column_of(half_own, 64)
    own = p[h, pl.ds(pl.multiple_of(384 + 64 * side, 64), 64), :]
    keys = jnp.concatenate([own[:, INNER : 2 * INNER], far[:, :INNER], near[:, :INNER], cross[:, :INNER]], axis=0)
    values = jnp.concatenate([own[:, 2 * INNER :], far[:, INNER:], near[:, INNER:], cross[:, INNER:]], axis=0)
    return attend(own[:, :INNER], keys, values, allowed)


def edge_ranks(h, side, corner, beside, own_strip, dn):
    mine = get_ranks(own_strip[1024:1040, :])
    above = dn[512:528, 768:1024].astype(F32)[0:1]
    return jnp.where(side == 0, corner, above) if h == 0 else jnp.where(side == 0, beside, mine)


def strips_kernel(first, second, w_ref, own_strip, dn, p_early, p_late, kve, tie, kvf, done):
    del tie
    tokens = jnp.concatenate([get_tokens(first, 128, 0, 128), get_tokens(second, 256, 0, 256)], axis=0)
    kv = jnp.dot(tokens, w_ref[:, INNER:], preferred_element_type=F32).astype(BF)
    kvf[0] = kv[0:64]
    kvf[1] = kv[64:128]
    side = 1 - lax.rem(lax.axis_index("cols"), 2)
    corner, beside = get_ranks(second[2064:2080, :]), get_ranks(second[2048:2064, :])

    def windows(p):
        for h in range(2):
            ranks = edge_ranks(h, side, corner, beside, own_strip, dn)
            far, cross = kv[128 + 64 * h : 192 + 64 * h], kv[256 + 64 * h : 320 + 64 * h]
            done[h] = edge_window(h, side, ranks, p, kve[h, side], far, cross)

    by_side(windows, p_early, p_late)


def edge_kernel(
    up, down, first, kvf, done, w_ref, own_strip, dn, p_early, p_late, inner, kve, out_hbm, edge, out, sem
):
    diags = jnp.concatenate([get_tokens(down, 64, 0, 64), get_tokens(up, 64, 0, 64)], axis=0)
    kvd = jnp.dot(diags, w_ref[:, INNER:], preferred_element_type=F32).astype(BF)
    corner, beside = get_ranks(down[512:528, :]), get_ranks(first[1024:1040, :])
    copies = [pltpu.make_async_copy(out.at[pl.ds(8 * h, 8)], out_hbm.at[pl.ds(8 * h, 8)], sem.at[h]) for h in range(2)]
    side = lax.rem(lax.axis_index("cols"), 2)

    def windows(p):
        for h in range(2):
            ranks = edge_ranks(h, side, corner, beside, own_strip, dn)
            edge[side] = edge_window(h, side, ranks, p, kve[h, side], kvf[h], kvd[64 * h : 64 * h + 64])
            edge[1 - side] = done[h]
            for i in range(HALF):
                row = [edge[0, 8 * i : 8 * i + 8]]
                row += [inner[h, j, 16 * i : 16 * i + 16].astype(F32) for j in range(3)]
                row += [edge[1, 8 * i : 8 * i + 8]]
                out[h * HALF + i] = jnp.concatenate(row, axis=0).astype(BF)
            copies[h].start()
        for copy in copies:
            copy.wait()

    by_side(windows, p_early, p_late)


SPLIT_FLOPS = 10000000000
VMEM = pl.BlockSpec(memory_space=pltpu.VMEM)
ANY = pl.BlockSpec(memory_space=pl.ANY)
HBM = pl.BlockSpec(memory_space=pltpu.HBM)


def call(kernel, outs, args, flops, anywhere=(), scratch=(), aliases=None, limit=24, held=(), to_hbm=False):
    single = len(outs) == 1
    return pl.pallas_call(
        kernel,
        out_shape=outs[0] if single else tuple(outs),
        in_specs=[HBM if i in held else ANY if i in anywhere else VMEM for i in range(len(args))],
        out_specs=HBM if to_hbm else VMEM if single else tuple([VMEM] * len(outs)),
        scratch_shapes=list(scratch),
        input_output_aliases=aliases or {},
        compiler_params=pltpu.CompilerParams(vmem_limit_bytes=limit * MIB),
        cost_estimate=pl.CostEstimate(flops=flops, bytes_accessed=1_000, transcendentals=0),
    )(*args)


def arr(*shape):
    return jax.ShapeDtypeStruct(shape, BF)


def along_rows(value, by):
    size = lax.axis_size("rows")
    return lax.ppermute(value, "rows", [(i, (i + by) % size) for i in range(size)])


def fixed(x):
    return pltpu.with_memory_space_constraint(x, pltpu.HBM)


def per_device(features, qkv_weight, orders):
    cols = lax.axis_size("cols")
    half = cols // 2
    up, dn, e1, e2 = call(
        pack_kernel,
        [arr(512, D), arr(528, D), arr(1040, 128), arr(1040, 128)],
        [fixed(features), fixed(orders)],
        1_000,
        held=(0, 1),
        scratch=[pltpu.VMEM((16, 64, D), BF), pltpu.VMEM((1, 4, 256), jnp.int32), pltpu.SemaphoreType.DMA((5,))],
        limit=16,
    )
    first = [(c, (c + 1) % cols if c % 2 else (c - 1) % cols) for c in range(cols)]
    second = [(c, (c - 1) % cols if c % 2 else (c + 1) % cols) for c in range(cols)]
    to_late = [(a, b) for a, b in first if a < half <= b]
    far = [b for _, b in to_late]
    got_x = lax.ppermute(e1, "cols", [pair for pair in first if pair not in to_late])
    got_up = along_rows(up, -1)
    got_dn = along_rows(dn, 1)
    p_early, again = call(
        project_early_kernel,
        [arr(2, 512, 3 * INNER), arr(1040, 128)],
        [up, dn, e1, fixed(qkv_weight)],
        1_000,
        held=(3,),
        scratch=[pltpu.VMEM((D, 3 * INNER), BF), pltpu.SemaphoreType.DMA((3,))],
    )
    got_y = lax.ppermute(again, "cols", to_late)
    p_late = call(
        project_late_kernel, [arr(2, 512, 3 * INNER)], [up, dn, qkv_weight, again], 1_000, anywhere=(3,)
    )
    z = call(gather_kernel, [arr(2080, 128)], [e2, got_up, got_dn], 1_000)
    got_z = lax.ppermute(z, "cols", second)
    inner, kve = call(
        inner_kernel,
        [arr(2, 3, 128, INNER), arr(2, 2, 64, 2 * INNER)],
        [got_up, got_dn, p_early, p_late, qkv_weight, orders, z],
        1_000,
        anywhere=(6,),
    )
    got_x = call(hold_kernel, [arr(1040, 128)], [got_x, kve], 1_000, anywhere=(1,))
    got_e1 = call(functools.partial(choose_kernel, far), [arr(1040, 128)], [got_x, got_y], 1_000)
    to_up, to_dn = call(split_kernel, [arr(512, 128), arr(528, 128)], [got_e1], SPLIT_FLOPS)
    hop_up = along_rows(to_up, -1)
    hop_dn = along_rows(to_dn, 1)
    kvf, done = call(
        strips_kernel,
        [arr(2, 64, 2 * INNER), jax.ShapeDtypeStruct((2, 64, INNER), F32)],
        [got_e1, got_z, qkv_weight, e1, got_dn, p_early, p_late, kve, to_up],
        1_000,
        anywhere=(8,),
    )
    return call(
        edge_kernel,
        [arr(16, 64, INNER)],
        [hop_up, hop_dn, got_e1, kvf, done, qkv_weight, e1, got_dn, p_early, p_late, inner, kve],
        1_000,
        scratch=[pltpu.VMEM((2, 64, INNER), F32), pltpu.VMEM((16, 64, INNER), BF), pltpu.SemaphoreType.DMA((2,))],
        to_hbm=True,
    )


def solution(mesh):
    in_specs = (P(("batch", "rows"), "cols", None), P(), P(("batch", "rows"), "cols", None))
    out_specs = P(("batch", "rows"), "cols", None)
    return jax.shard_map(
        per_device, mesh=mesh, in_specs=in_specs, out_specs=out_specs, check_vma=False
    )
```

```python
import functools

import jax
import jax.numpy as jnp
from jax import lax
from jax.experimental import pallas as pl
from jax.experimental.pallas import tpu as pltpu
from jax.sharding import PartitionSpec as P

D = 1024
HEADS = 8
HEAD_DIM = 64
INNER = 512
HALF = 8
EPSILON = 1e-06
LOG2E = 1.4426950408889634
FAR = 4096.0
BF = jnp.bfloat16
F32 = jnp.float32
MIB = 1 << 20


def normalize(values):
    center = jnp.mean(values, axis=-1, keepdims=True)
    off = values - center
    spread = jnp.mean(off * off, axis=-1, keepdims=True)
    return off * lax.rsqrt(spread + EPSILON)


def put_tokens(ref, per, at, values):
    for k in range(8):
        ref[per * k + at : per * k + at + values.shape[0], :] = values[:, 128 * k : 128 * k + 128]


def get_tokens(ref, per, at, count):
    return jnp.concatenate([ref[per * k + at : per * k + at + count, :] for k in range(8)], axis=1)


def get_ranks(block):
    block = block.astype(F32)
    return jnp.concatenate([block[0:1], block[8:9]], axis=1)


def store_ranks(ord_ref, dn, strips):
    ranks = ord_ref[0].astype(F32).astype(BF)
    natural = lax.broadcasted_iota(jnp.int32, (256, 256), 0)
    m = lax.broadcasted_iota(jnp.int32, (256, 256), 1)
    source = ((m >> 7) * 8 + ((m >> 3) & 7)) * 16 + ((m >> 6) & 1) * 8 + (m & 7)
    quads = jnp.dot(ranks, (natural == source).astype(F32).astype(BF), preferred_element_type=F32)
    rank_row = jnp.concatenate(
        [ranks[0:1].astype(F32), ranks[1:2].astype(F32), ranks[2:3].astype(F32), quads[3:4]], axis=1
    )
    dn[512:528, :] = jnp.broadcast_to(rank_row, (16, D)).astype(BF)
    halves = [jnp.broadcast_to(quads[3:4, 128 * n : 128 * n + 128], (8, 128)) for n in range(2)]
    for ref in strips:
        ref[1024:1040, :] = jnp.concatenate(halves, axis=0).astype(BF)


def put_strips(odd, at, left, right, e1, e2):
    put_tokens(e1, 128, at, jnp.where(odd, right, left))
    put_tokens(e2, 128, at, jnp.where(odd, left, right))


def pack_rows(x_ref, ord_hbm, up, dn, held, ord_ref, sem, strips=()):
    odd = lax.rem(lax.axis_index("cols"), 2) == 1
    copies = [
        pltpu.make_async_copy(x_ref.at[pl.ds(4 * q, 4)], held.at[pl.ds(4 * q, 4)], sem.at[q]) for q in range(4)
    ]
    ranks_copy = pltpu.make_async_copy(ord_hbm, ord_ref, sem.at[4])
    ranks_copy.start()
    for copy in copies:
        copy.start()
    ranks_copy.wait()
    store_ranks(ord_ref, dn, strips)
    for q in range(8):
        if q % 2 == 0:
            copies[q // 2].wait()
        h, t = q // 4, q % 4
        ref = dn if h else up
        lefts, rights = [], []
        for u in range(2):
            before = None
            for k in range(4):
                part = normalize(held[2 * q + u, 16 * k : 16 * k + 16, :].astype(F32))
                if k == 0:
                    lefts.append(part[:8])
                else:
                    at = 128 * (k - 1) + (2 * t + u) * 16
                    ref[at : at + 16, :] = jnp.concatenate([before, part[:8]], axis=0).astype(BF)
                before = part[8:]
            rights.append(before)
        left = jnp.concatenate(lefts, axis=0).astype(BF)
        right = jnp.concatenate(rights, axis=0).astype(BF)
        ref[384 + t * 16 : 400 + t * 16, :] = left
        ref[448 + t * 16 : 464 + t * 16, :] = right
        put_strips(odd, 64 * h + t * 16, left, right, *strips)


def pack_kernel(x_ref, ord_hbm, up, dn, e1, e2, held, ord_ref, sem):
    pack_rows(x_ref, ord_hbm, up, dn, held, ord_ref, sem, (e1, e2))


def is_early():
    return lax.axis_index("cols") < lax.axis_size("cols") // 2


def project_early_kernel(up, dn, e1, w_hbm, p, e1_again, w_ref, sem):
    @pl.when(is_early())
    def _():
        e1_again[...] = e1[...]
        copies = []
        for n in range(3):
            at = pl.ds(INNER * n, INNER)
            copies.append(pltpu.make_async_copy(w_hbm.at[:, at], w_ref.at[:, at], sem.at[n]))
        for copy in copies:
            copy.start()
        for n, copy in enumerate(copies):
            copy.wait()
            at = slice(INNER * n, INNER * n + INNER)
            for h, src in enumerate((up, dn)):
                p[h, :, at] = jnp.dot(src[0:512, :], w_ref[:, at], preferred_element_type=F32).astype(BF)


def hold_kernel(value, tie, same):
    del tie
    same[...] = value[...]


def project_late_kernel(up, dn, w_ref, tie, p):
    del tie

    @pl.when(jnp.logical_not(is_early()))
    def _():
        for h, src in enumerate((up, dn)):
            for q in range(2):
                at = slice(256 * q, 256 * q + 256)
                p[h, at, :] = jnp.dot(src[at, :], w_ref[...], preferred_element_type=F32).astype(BF)


def column_of(row, count):
    q = lax.broadcasted_iota(jnp.int32, (count, 128), 0)
    lane = lax.broadcasted_iota(jnp.int32, (count, 128), 1)
    return jnp.sum(jnp.where(q == lane, jnp.broadcast_to(row, (count, 128)), 0.0), axis=1, keepdims=True)


def attend(query, keys, values, allowed):
    count = query.shape[0]
    both = jnp.concatenate([allowed, allowed], axis=0)
    first = lax.broadcasted_iota(jnp.int32, (count, 128), 1) < HEAD_DIM
    ones = jnp.ones((256, 128), BF)
    outs = []
    for g in range(4):
        at = slice(128 * g, 128 * g + 128)
        q = query[:, at]
        zero = jnp.zeros_like(q)
        q = jnp.concatenate([jnp.where(first, q, zero), jnp.where(first, zero, q)], axis=0)
        s = lax.dot_general(q, keys[:, at], (((1,), (1,)), ((), ())), preferred_element_type=F32)
        s = jnp.where(both, s, -jnp.inf)
        top = jnp.max(s, axis=-1, keepdims=True)
        p = jnp.exp2((s - top) * (LOG2E * HEAD_DIM**-0.5)).astype(BF)
        o = jnp.dot(p, jnp.concatenate([values[:, at], ones], axis=1), preferred_element_type=F32)
        number = jnp.where(first, o[:count, :128], o[count:, :128])
        total = jnp.where(first, o[:count, 128:], o[count:, 128:])
        outs.append(number / total)
    return jnp.concatenate(outs, axis=1)


def inner_window(h, j, own, other_kv, rank_row, last, out):
    own_ranks = rank_row[:, 128:] if h == 0 else rank_row[:, :128]
    other_ranks = (rank_row[:, :128] if h == 0 else rank_row[:, 128:]) + jnp.where(last, FAR, 0.0)
    key_ranks = jnp.concatenate([own_ranks, other_ranks], axis=1)
    allowed = key_ranks <= column_of(own_ranks, 128)
    keys = jnp.concatenate([own[:, INNER : 2 * INNER], other_kv[:, :INNER]], axis=0)
    values = jnp.concatenate([own[:, 2 * INNER :], other_kv[:, INNER:]], axis=0)
    out[h, j] = attend(own[:, :INNER], keys, values, allowed).astype(BF)


def last_pair(h):
    size = lax.axis_size("rows")
    return lax.axis_index("rows") == (0 if h == 0 else size - 1)


def by_side(body, p_early, p_late):
    early = is_early()
    pl.when(early)(lambda: body(p_early))
    pl.when(jnp.logical_not(early))(lambda: body(p_late))


def inner_kernel(up, dn, p_early, p_late, w_ref, ord_ref, tie, out, kve):
    del tie
    by_side(lambda p: inner_windows(up, dn, p, w_ref, ord_ref, out, kve), p_early, p_late)


def inner_windows(up, dn, p, w_ref, ord_ref, out, kve):
    for h, src in enumerate((dn, up)):
        kv = jnp.dot(src[0:512, :], w_ref[:, INNER:], preferred_element_type=F32).astype(BF)
        for j in range(3):
            if h == 0:
                ranks = dn[512:528, 256 * j : 256 * j + 256].astype(F32)[0:1]
            else:
                ranks = ord_ref[0, j : j + 1, :].astype(F32)
            at = slice(128 * j, 128 * j + 128)
            inner_window(h, j, p[h, at, :], kv[at], ranks, last_pair(h), out)
        kve[h, 0] = kv[384:448]
        kve[h, 1] = kv[448:512]


def one_of(cols):
    col = lax.axis_index("cols")
    return functools.reduce(jnp.logical_or, [col == c for c in cols])


def choose_kernel(far, got_x, got_y, e1, to_up, to_dn):
    from_y = one_of(far)
    for src, wanted in ((got_x, jnp.logical_not(from_y)), (got_y, from_y)):

        @pl.when(wanted)
        def _(src=src):
            e1[...] = src[...]
            put_tokens(to_up, 64, 0, get_tokens(src, 128, 0, 64))
            put_tokens(to_dn, 64, 0, get_tokens(src, 128, 64, 64))
            to_dn[512:528, :] = src[1024:1040, :]


def gather_kernel(e2, got_up, got_dn, z):
    odd = lax.rem(lax.axis_index("cols"), 2)
    at = pl.ds(pl.multiple_of(384 + 64 * (1 - odd), 64), 64)
    put_tokens(z, 256, 0, get_tokens(e2, 128, 0, 128))
    put_tokens(z, 256, 128, got_dn[at, :])
    put_tokens(z, 256, 192, got_up[at, :])
    z[2048:2064, :] = e2[1024:1040, :]
    ranks = got_dn[512:528, 768:1024].astype(F32)
    z[2064:2080, :] = jnp.concatenate([ranks[0:8, :128], ranks[8:16, 128:]], axis=0).astype(BF)


def edge_window(h, side, ranks, p, near, far, cross):
    col = lax.axis_index("cols")
    lane = lax.broadcasted_iota(jnp.int32, (1, 128), 1)
    is_left = side == 0
    last_col = jnp.where(is_left, col == 0, col == lax.axis_size("cols") - 1)
    half_own = ranks[:, 128:] if h == 0 else ranks[:, :128]
    half_other = ranks[:, :128] if h == 0 else ranks[:, 128:]
    half_own, half_other = (
        jnp.where(is_left, jnp.concatenate([x[:, 64:], x[:, :64]], axis=1), x) for x in (half_own, half_other)
    )
    far_col = jnp.where((lane >= 64) & last_col, FAR, 0.0)
    key_ranks = jnp.concatenate([half_own + far_col, half_other + far_col + jnp.where(last_pair(h), FAR, 0.0)], axis=1)
    allowed = key_ranks <= column_of(half_own, 64)
    own = p[h, pl.ds(pl.multiple_of(384 + 64 * side, 64), 64), :]
    keys = jnp.concatenate([own[:, INNER : 2 * INNER], far[:, :INNER], near[:, :INNER], cross[:, :INNER]], axis=0)
    values = jnp.concatenate([own[:, 2 * INNER :], far[:, INNER:], near[:, INNER:], cross[:, INNER:]], axis=0)
    return attend(own[:, :INNER], keys, values, allowed)


def edge_ranks(h, side, corner, beside, own_strip, dn):
    mine = get_ranks(own_strip[1024:1040, :])
    above = dn[512:528, 768:1024].astype(F32)[0:1]
    return jnp.where(side == 0, corner, above) if h == 0 else jnp.where(side == 0, beside, mine)


def strips_kernel(first, second, w_ref, own_strip, dn, p_early, p_late, kve, tie, kvf, done):
    del tie
    tokens = jnp.concatenate([get_tokens(first, 128, 0, 128), get_tokens(second, 256, 0, 256)], axis=0)
    kv = jnp.dot(tokens, w_ref[:, INNER:], preferred_element_type=F32).astype(BF)
    kvf[0] = kv[0:64]
    kvf[1] = kv[64:128]
    side = 1 - lax.rem(lax.axis_index("cols"), 2)
    corner, beside = get_ranks(second[2064:2080, :]), get_ranks(second[2048:2064, :])

    def windows(p):
        for h in range(2):
            ranks = edge_ranks(h, side, corner, beside, own_strip, dn)
            far, cross = kv[128 + 64 * h : 192 + 64 * h], kv[256 + 64 * h : 320 + 64 * h]
            done[h] = edge_window(h, side, ranks, p, kve[h, side], far, cross)

    by_side(windows, p_early, p_late)


def edge_kernel(
    up, down, first, kvf, done, w_ref, own_strip, dn, p_early, p_late, inner, kve, out_hbm, edge, out, sem
):
    diags = jnp.concatenate([get_tokens(down, 64, 0, 64), get_tokens(up, 64, 0, 64)], axis=0)
    kvd = jnp.dot(diags, w_ref[:, INNER:], preferred_element_type=F32).astype(BF)
    corner, beside = get_ranks(down[512:528, :]), get_ranks(first[1024:1040, :])
    copies = [pltpu.make_async_copy(out.at[pl.ds(8 * h, 8)], out_hbm.at[pl.ds(8 * h, 8)], sem.at[h]) for h in range(2)]
    side = lax.rem(lax.axis_index("cols"), 2)

    def windows(p):
        for h in range(2):
            ranks = edge_ranks(h, side, corner, beside, own_strip, dn)
            edge[side] = edge_window(h, side, ranks, p, kve[h, side], kvf[h], kvd[64 * h : 64 * h + 64])
            edge[1 - side] = done[h]
            for i in range(HALF):
                row = [edge[0, 8 * i : 8 * i + 8]]
                row += [inner[h, j, 16 * i : 16 * i + 16].astype(F32) for j in range(3)]
                row += [edge[1, 8 * i : 8 * i + 8]]
                out[h * HALF + i] = jnp.concatenate(row, axis=0).astype(BF)
            copies[h].start()
        for copy in copies:
            copy.wait()

    by_side(windows, p_early, p_late)


SPLIT_FLOPS = 10000000000
VMEM = pl.BlockSpec(memory_space=pltpu.VMEM)
ANY = pl.BlockSpec(memory_space=pl.ANY)
HBM = pl.BlockSpec(memory_space=pltpu.HBM)


def call(kernel, outs, args, flops, anywhere=(), scratch=(), aliases=None, limit=24, held=(), to_hbm=False):
    single = len(outs) == 1
    return pl.pallas_call(
        kernel,
        out_shape=outs[0] if single else tuple(outs),
        in_specs=[HBM if i in held else ANY if i in anywhere else VMEM for i in range(len(args))],
        out_specs=HBM if to_hbm else VMEM if single else tuple([VMEM] * len(outs)),
        scratch_shapes=list(scratch),
        input_output_aliases=aliases or {},
        compiler_params=pltpu.CompilerParams(vmem_limit_bytes=limit * MIB),
        cost_estimate=pl.CostEstimate(flops=flops, bytes_accessed=1_000, transcendentals=0),
    )(*args)


def arr(*shape):
    return jax.ShapeDtypeStruct(shape, BF)


def along_rows(value, by):
    size = lax.axis_size("rows")
    return lax.ppermute(value, "rows", [(i, (i + by) % size) for i in range(size)])


def fixed(x):
    return pltpu.with_memory_space_constraint(x, pltpu.HBM)


def per_device(features, qkv_weight, orders):
    cols = lax.axis_size("cols")
    half = cols // 2
    up, dn, e1, e2 = call(
        pack_kernel,
        [arr(512, D), arr(528, D), arr(1040, 128), arr(1040, 128)],
        [fixed(features), fixed(orders)],
        1_000,
        held=(0, 1),
        scratch=[pltpu.VMEM((16, 64, D), BF), pltpu.VMEM((1, 4, 256), jnp.int32), pltpu.SemaphoreType.DMA((5,))],
        limit=16,
    )
    first = [(c, (c + 1) % cols if c % 2 else (c - 1) % cols) for c in range(cols)]
    second = [(c, (c - 1) % cols if c % 2 else (c + 1) % cols) for c in range(cols)]
    to_late = [(a, b) for a, b in first if a < half <= b]
    far = [b for _, b in to_late]
    got_x = lax.ppermute(e1, "cols", [pair for pair in first if pair not in to_late])
    got_up = along_rows(up, -1)
    got_dn = along_rows(dn, 1)
    p_early, again = call(
        project_early_kernel,
        [arr(2, 512, 3 * INNER), arr(1040, 128)],
        [up, dn, e1, fixed(qkv_weight)],
        1_000,
        held=(3,),
        scratch=[pltpu.VMEM((D, 3 * INNER), BF), pltpu.SemaphoreType.DMA((3,))],
    )
    got_y = lax.ppermute(again, "cols", to_late)
    p_late = call(
        project_late_kernel, [arr(2, 512, 3 * INNER)], [up, dn, qkv_weight, again], 1_000, anywhere=(3,)
    )
    z = call(gather_kernel, [arr(2080, 128)], [e2, got_up, got_dn], 1_000)
    got_z = lax.ppermute(z, "cols", second)
    inner, kve = call(
        inner_kernel,
        [arr(2, 3, 128, INNER), arr(2, 2, 64, 2 * INNER)],
        [got_up, got_dn, p_early, p_late, qkv_weight, orders, z],
        1_000,
        anywhere=(6,),
    )
    got_x = call(hold_kernel, [arr(1040, 128)], [got_x, kve], 1_000, anywhere=(1,))
    got_e1, to_up, to_dn = call(
        functools.partial(choose_kernel, far),
        [arr(1040, 128), arr(512, 128), arr(528, 128)],
        [got_x, got_y],
        SPLIT_FLOPS,
    )
    hop_up = along_rows(to_up, -1)
    hop_dn = along_rows(to_dn, 1)
    kvf, done = call(
        strips_kernel,
        [arr(2, 64, 2 * INNER), jax.ShapeDtypeStruct((2, 64, INNER), F32)],
        [got_e1, got_z, qkv_weight, e1, got_dn, p_early, p_late, kve, to_up],
        1_000,
        anywhere=(8,),
    )
    return call(
        edge_kernel,
        [arr(16, 64, INNER)],
        [hop_up, hop_dn, got_e1, kvf, done, qkv_weight, e1, got_dn, p_early, p_late, inner, kve],
        1_000,
        scratch=[pltpu.VMEM((2, 64, INNER), F32), pltpu.VMEM((16, 64, INNER), BF), pltpu.SemaphoreType.DMA((2,))],
        to_hbm=True,
    )


def solution(mesh):
    in_specs = (P(("batch", "rows"), "cols", None), P(), P(("batch", "rows"), "cols", None))
    out_specs = P(("batch", "rows"), "cols", None)
    return jax.shard_map(
        per_device, mesh=mesh, in_specs=in_specs, out_specs=out_specs, check_vma=False
    )
```
